128 devices in a mesh: group: 8 (over y, core), member: 16 (over z, x).
Axes of the slice: x: 4, y: 4, z: 4, core: 2. Of those that a mesh axis runs over, the one named last changes fastest.
Arguments:
- hot_table: float32 [32768, 128], P('member'), may hold values from -6 to 6
- hot_acc: float32 [32768], P('member'), may hold values from 0.05 to 0.5
- cold_table: float32 [524288, 128], P(('group', 'member')), may hold values from -6 to 6
- cold_acc: float32 [524288], P(('group', 'member')), may hold values from 0.05 to 0.5
- bottom_out: bfloat16 [16384, 128], P(('group', 'member')), may hold values from -6 to 6
- labels: float32 [16384], P(('group', 'member')), may hold values from 0 to 1
- hot_owner: int32 [16384, 8, 2], P(('group', 'member')), may hold values from 0 to 15, all different within a row; in each aligned block of 1024 rows (0 to 1023, 1024 to 2047, ..., all dimensions but the last counted through in order) at most 256 rows name the same one
- hot_offset: int32 [16384, 8, 2], P(('group', 'member')), may hold values from 0 to 2047
- cold_owner: int32 [16384, 8, 1], P(('group', 'member')), may hold values from 0 to 127; in each aligned block of 1024 rows (0 to 1023, 1024 to 2047, ..., all dimensions but the last counted through in order) at most 32 rows name the same one
- cold_offset: int32 [16384, 8, 1], P(('group', 'member')), may hold values from 0 to 4095
- w_first: bfloat16 [1152, 2048], replicated, may hold values from -0.25 to 0.25
- w_second: bfloat16 [2048, 2048], replicated, may hold values from -0.1875 to 0.1875
- w_out: bfloat16 [2048], replicated, may hold values from -0.25 to 0.25
Outputs:
- new_hot: float32 [32768, 128], P('member')
- new_hot_acc: float32 [32768], P('member')
- new_cold: float32 [524288, 128], P(('group', 'member'))
- new_cold_acc: float32 [524288], P(('group', 'member'))
The draws below stay inside these ranges and needn't reach their ends.
Inputs may be any that keep to these rules, and one draw needn't show every extreme that they name: `hot_owner`: the 2 entries of one sample and table differ. Among the 1024 sample-table pairs of one device, no member is named by more than 256 pairs, a bound that some block reaches. `cold_owner`: devices are numbered along group+member. Among the 1024 sample-table pairs of one device, no device is named by more than 32 pairs, and some device by exactly 32.
All inputs are finite; a program needn't handle non-finite values.
Results may differ from the reference program's by a relative error of at most 0.012.
Values may be sent and summed in bfloat16 or wider, within the bound.
A program may use at most 128 MiB of HBM per device.

```python
import math
import jax
import jax.numpy as jnp
import numpy as np
from jax import lax

E = 128
H = 2048
F = 8
LH = 2
LC = 1
B_DEV = 128
HOT_DEV = 2048
COLD_DEV = 4096
HCAP = 256
CCAP = 32
BATCH = 16384
HOT = 32768
COLD = 524288
N_MEMBER = 16
DEVICES = 128


def place_ends(result, own_key, low, largest):
    spot = [jax.random.randint(jax.random.fold_in(own_key, axis), (), 0, length) for axis, length in enumerate(result.shape)]
    main_axis = result.shape.index(max(result.shape))
    beside = spot[:main_axis] + [(spot[main_axis] + 1) % result.shape[main_axis]] + spot[main_axis + 1:]
    return result.at[tuple(spot)].set(low).at[tuple(beside)].set(largest)


def block_levels(own_key, extent, shards, smallest, top_value):
    loudness, own = 1.0, jax.random.fold_in(own_key, 6)
    for position, parts in shards:
        draws = jnp.exp(jax.random.uniform(jax.random.fold_in(own, position), (parts,), jnp.float32, smallest / len(shards), top_value / len(shards)))
        loudness = loudness * jnp.repeat(draws, extent[position] // parts).reshape([-1 if axis == position else 1 for axis in range(len(extent))])
    return loudness


def deal_out(key, own, number, rows, count, top, limit, slope):
    order = jax.random.permutation(key, count)
    heavy_load, ordinary = shares(count, rows * top, limit, slope, True), shares(count, rows * top, limit, slope, False)
    places = jnp.arange(count)

    def named(sizes, offset_by):
        used = int((sizes > 0).sum())
        fixed = max(1, used // 4)
        shifted = fixed + (places - fixed + offset_by * (used - fixed)) % max(1, count - fixed)
        return jnp.zeros((count,), jnp.int32).at[order[jnp.where(places < fixed, places, shifted)]].set(jnp.asarray(sizes, jnp.int32))

    sizes = jnp.where(number % 4 == 0, named(heavy_load, number // 4), named(ordinary, number - number // 4 - 1))
    mixed = jax.random.permutation(jax.random.fold_in(own, 3), count)
    giver, taker = mixed[0:count // 2 * 2:2], mixed[1:count // 2 * 2:2]
    slack = jnp.minimum(sizes[giver] - 1, limit - sizes[taker]) // 2
    slack = jnp.where((giver == order[0]) | (taker == order[0]) | (sizes[taker] == 0), 0, jnp.maximum(slack, 0))
    shifted = jax.random.randint(jax.random.fold_in(own, 4), (count // 2,), 0, 1 << 20) % (slack + 1)
    sizes = sizes.at[giver].add(-shifted).at[taker].add(shifted)
    items = jnp.searchsorted(jnp.cumsum(sizes), jnp.arange(rows * top), side="right").astype(jnp.int32)
    grid = items.reshape(top, rows).T
    grid = grid[jax.random.permutation(jax.random.fold_in(own, 1), rows)]
    offset_by = jax.random.randint(jax.random.fold_in(own, 2), (rows, 1), 0, top)
    return jnp.take_along_axis(grid, (jnp.arange(top)[None, :] + offset_by) % top, axis=1)


def shares(number_of, total, most, lean, full):
    loads = [(1 << 20) // math.isqrt(standing ** lean) + 1 for standing in range(1, number_of + 1)]
    largest = most if full else min(most, max(-(-total // number_of), total * loads[0] // sum(loads)))
    least = 1 if total - largest >= number_of - 1 else 0
    given, spare = [largest] + [least] * (number_of - 1), total - largest - least * (number_of - 1)
    while spare > 0:
        candidates = [i for i in range(1, number_of) if given[i] < largest] or [i for i in range(1, number_of) if given[i] < most]
        mass, budget = sum([loads[i] for i in candidates]), spare
        for i in candidates:
            more = min(most - given[i], max(1, budget * loads[i] // mass), spare)
            given[i] = given[i] + more
            spare = spare - more
    return np.array(given)


def scatter_about(rng, extent, spread, limit, shards=(), held_as=jnp.bfloat16):
    factor_of = block_levels(rng, extent, shards, -0.22, 0.18) if shards else 1.0
    drawn = jax.random.normal(rng, extent, jnp.float32) * spread * factor_of
    return jnp.minimum(jnp.maximum(drawn, -limit), limit).astype(held_as)


def setup_inputs(seed: int = 0) -> dict:
    splits = jax.random.split(jax.random.key(seed), 14)
    hot_table = scatter_about(splits[0], (HOT, E), 1.0, 6.0, ((0, 16),), jnp.float32)
    hot_acc = jnp.clip(jnp.exp(math.log(0.5) - 2.3025851 * jax.random.uniform(splits[1], (HOT,), jnp.float32) ** block_levels(splits[1], (HOT,), ((0, 16),), -0.2, 0.2)), 0.05, 0.5)
    cold_table = scatter_about(splits[2], (COLD, E), 1.0, 6.0, ((0, 128),), jnp.float32)
    cold_acc = jnp.clip(jnp.exp(math.log(0.5) - 2.3025851 * jax.random.uniform(splits[3], (COLD,), jnp.float32) ** block_levels(splits[3], (COLD,), ((0, 128),), -0.2, 0.2)), 0.05, 0.5)
    bottom_out = scatter_about(splits[4], (BATCH, E), 1.0, 6.0, ((0, 128),))
    labels = jnp.clip(1.0 * jax.random.uniform(splits[5], (BATCH,), jnp.float32) ** block_levels(splits[5], (BATCH,), ((0, 128),), -0.2, 0.2), 0.0, 1.0)
    hot_owner_keys = jax.random.split(jax.random.fold_in(splits[6], 1), BATCH * F // (B_DEV * F))
    hot_owner_turns = jax.random.permutation(jax.random.fold_in(splits[6], 3), BATCH * F // (B_DEV * F))
    hot_owner = jax.vmap(lambda own, number: deal_out(jax.random.fold_in(splits[6], 2), own, number, B_DEV * F, N_MEMBER, LH, HCAP, 2))(hot_owner_keys, hot_owner_turns).reshape((BATCH, F, LH))
    hot_offset = place_ends(jax.random.randint(splits[7], (BATCH, F, LH), 0, HOT_DEV), jax.random.fold_in(splits[7], 1), 0, HOT_DEV - 1).astype(jnp.int32)
    cold_owner_keys = jax.random.split(jax.random.fold_in(splits[8], 1), BATCH * F // (B_DEV * F))
    cold_owner_turns = jax.random.permutation(jax.random.fold_in(splits[8], 3), BATCH * F // (B_DEV * F))
    cold_owner = jax.vmap(lambda own, number: deal_out(jax.random.fold_in(splits[8], 2), own, number, B_DEV * F, DEVICES, LC, CCAP, 2))(cold_owner_keys, cold_owner_turns).reshape((BATCH, F, LC))
    cold_offset = place_ends(jax.random.randint(splits[9], (BATCH, F, LC), 0, COLD_DEV), jax.random.fold_in(splits[9], 1), 0, COLD_DEV - 1).astype(jnp.int32)
    w_first = scatter_about(splits[10], ((F + 1) * E, H), ((F + 1) * E // 2) ** -0.5, 0.25)
    w_second = scatter_about(splits[11], (H, H), (H // 2) ** -0.5, 0.1875)
    w_out = scatter_about(splits[12], (H,), (H // 4) ** -0.5, 0.25)
    return dict(hot_table=hot_table, hot_acc=hot_acc, cold_table=cold_table, cold_acc=cold_acc, bottom_out=bottom_out, labels=labels, hot_owner=hot_owner, hot_offset=hot_offset, cold_owner=cold_owner, cold_offset=cold_offset, w_first=w_first, w_second=w_second, w_out=w_out)


STEP_RATE = 0.5

def reference(hot_table, hot_acc, cold_table, cold_acc, bottom_out, labels, hot_owner, hot_offset, cold_owner, cold_offset, w_first, w_second, w_out):
    row_width = hot_table.shape[1]
    blocks = BATCH // B_DEV

    def block_step(totals, block_items):
        hot_total, cold_total = totals
        bottom_block, label_block, hot_who, hot_off, cold_who, cold_off = block_items
        hot_index = (hot_who * HOT_DEV + hot_off).reshape(-1).astype(jnp.int32)
        cold_index = (cold_who * COLD_DEV + cold_off).reshape(-1).astype(jnp.int32)
        hot_vals = lax.optimization_barrier(hot_table[hot_index].astype(jnp.bfloat16))
        cold_vals = lax.optimization_barrier(cold_table[cold_index].astype(jnp.bfloat16))
        hot_vals = hot_vals.astype(jnp.float32).reshape(B_DEV, F, LH, row_width)
        cold_vals = cold_vals.astype(jnp.float32).reshape(B_DEV, F, LC, row_width)
        pooled = (lax.optimization_barrier(jnp.sum(hot_vals, axis=2)) + lax.optimization_barrier(jnp.sum(cold_vals, axis=2))).astype(jnp.bfloat16)
        features = jnp.concatenate([bottom_block, pooled.reshape(B_DEV, F * row_width)], axis=1)
        first_pre = jnp.dot(features, w_first, preferred_element_type=jnp.float32)
        first_act = jnp.maximum(first_pre, 0.0).astype(jnp.bfloat16)
        second_pre = jnp.dot(first_act, w_second, preferred_element_type=jnp.float32)
        second_act = jnp.maximum(second_pre, 0.0).astype(jnp.bfloat16)
        score = jnp.dot(second_act, w_out, preferred_element_type=jnp.float32)
        delta = jax.nn.sigmoid(score) - label_block
        grad_second = jnp.where(second_pre > 0, delta[:, None] * w_out.astype(jnp.float32)[None, :], 0.0).astype(jnp.bfloat16)
        back_second = jnp.dot(grad_second, w_second.T, preferred_element_type=jnp.float32)
        grad_first = jnp.where(first_pre > 0, back_second, 0.0).astype(jnp.bfloat16)
        grad_features = jnp.dot(grad_first, w_first.T, preferred_element_type=jnp.float32)
        grad_pooled = grad_features[:, row_width:].reshape(B_DEV, F, 1, row_width)
        hot_terms = jnp.broadcast_to(grad_pooled, (B_DEV, F, LH, row_width)).reshape(-1, row_width)
        cold_terms = jnp.broadcast_to(grad_pooled, (B_DEV, F, LC, row_width)).reshape(-1, row_width)
        return ((hot_total.at[hot_index].add(hot_terms), cold_total.at[cold_index].add(cold_terms)), None)
    block_items = (bottom_out.reshape(blocks, B_DEV, row_width), labels.reshape(blocks, B_DEV), hot_owner.reshape(blocks, B_DEV, F, LH), hot_offset.reshape(blocks, B_DEV, F, LH), cold_owner.reshape(blocks, B_DEV, F, LC), cold_offset.reshape(blocks, B_DEV, F, LC))
    start = (jnp.zeros(hot_table.shape, jnp.float32), jnp.zeros(cold_table.shape, jnp.float32))
    (hot_grad, cold_grad), unused = lax.scan(block_step, start, block_items)
    new_hot_acc = hot_acc + lax.optimization_barrier(jnp.mean(hot_grad * hot_grad, axis=1))
    new_cold_acc = cold_acc + lax.optimization_barrier(jnp.mean(cold_grad * cold_grad, axis=1))
    new_hot = hot_table - STEP_RATE * hot_grad / jnp.sqrt(new_hot_acc)[:, None]
    new_cold = cold_table - STEP_RATE * cold_grad / jnp.sqrt(new_cold_acc)[:, None]
    return (new_hot, new_hot_acc, new_cold, new_cold_acc)
```

```python
import functools
import jax
import jax.numpy as jnp
from jax import lax
from jax.experimental import pallas as pl
from jax.experimental.pallas import tpu as pltpu
from jax.sharding import PartitionSpec as P
V = pl.BlockSpec(memory_space=pltpu.VMEM)
S = pl.BlockSpec(memory_space=pltpu.SMEM)
BIG = pltpu.CompilerParams(vmem_limit_bytes=56 << 20)

def place_one(owner_ref, offset_ref, n, cap, req_ref, pos_ref):
    R = owner_ref.shape[0]
    own = lax.broadcasted_iota(jnp.int32, (n, 128), 0)
    masks = [(owner_ref[r:r + 1, :] == own) for r in range(R)]
    low = [m.astype(jnp.float32) for m in masks]
    stacked = jnp.concatenate(low, axis=0).astype(jnp.bfloat16)
    a = lax.broadcasted_iota(jnp.int32, (128, 128), 0)
    b = lax.broadcasted_iota(jnp.int32, (128, 128), 1)
    tri = (a < b).astype(jnp.float32)
    side = jnp.concatenate([tri, jnp.ones((128, 128), jnp.float32)], axis=1).astype(jnp.bfloat16)
    counts = jnp.dot(stacked, side, preferred_element_type=jnp.float32)
    base = jnp.zeros((n, 128), jnp.float32)
    his, los, hots = [], [], []
    capi = lax.broadcasted_iota(jnp.int32, (cap, 128), 0)
    for r in range(R):
        c = counts[r * n:(r + 1) * n]
        slot = jnp.sum(low[r] * (c[:, :128] + base), axis=0, keepdims=True).astype(jnp.int32)
        base = base + c[:, 128:]
        pos_ref[r:r + 1, :] = owner_ref[r:r + 1, :] * cap + slot
        off = offset_ref[r:r + 1, :]
        his.append(low[r] * (off // 64).astype(jnp.float32))
        los.append(low[r] * (off % 64).astype(jnp.float32))
        hots.append((capi == slot).astype(jnp.float32).astype(jnp.bfloat16))
    A = jnp.concatenate([jnp.concatenate(his, axis=1), jnp.concatenate(los, axis=1)], axis=0).astype(jnp.bfloat16)
    B = jnp.concatenate(hots, axis=1)
    got = lax.dot_general(A, B, (((1,), (1,)), ((), ())), preferred_element_type=jnp.float32)
    req_ref[...] = (got[:n] * 64.0 + got[n:]).astype(jnp.int32)

def place_kernel(ho, hf, co, cf, hreq, hpos, creq, cpos):
    place_one(ho, hf, 16, 256, hreq, hpos)
    place_one(co, cf, 128, 32, creq, cpos)

def place(ho, hf, co, cf):
    return pl.pallas_call(place_kernel, out_shape=[jax.ShapeDtypeStruct(s, jnp.int32) for s in [(16,256),(16,128),(128,32),(8,128)]],
        in_specs=[V]*4, out_specs=[V]*4, compiler_params=BIG, name="place")(ho, hf, co, cf)

def serve_kernel(U, CH, idx_ref, tab_ref, out_ref, stage):
    n = out_ref.shape[0]
    def chunk(c, _):
        base = c * CH
        for j in range(CH):
            stage[pl.ds(j, 1), :] = tab_ref[pl.ds(idx_ref[base + j], 1), :]
        out_ref[pl.ds(pl.multiple_of(base, CH), CH), :] = stage[...].astype(jnp.bfloat16)
        return 0
    lax.fori_loop(0, n // CH, chunk, 0)

def serve(idx, tab, CH=32, U=8):
    return pl.pallas_call(functools.partial(serve_kernel, U, CH), out_shape=jax.ShapeDtypeStruct((idx.shape[0],128), jnp.bfloat16),
        in_specs=[S, V], out_specs=V, scratch_shapes=[pltpu.VMEM((CH,128), jnp.float32)], compiler_params=BIG, name="serve")(idx, tab)

def settle_kernel(BR, BK, idx_ref, val_ref, out_ref):
    rows = out_ref.shape[0]
    K = val_ref.shape[0]
    def blk(i, _):
        first = i * BR
        it = lax.broadcasted_iota(jnp.int32, (BR, BK), 0)
        acc = jnp.zeros((BR, 128), jnp.float32)
        for k in range(K // BK):
            rel = idx_ref[:, k * BK:(k + 1) * BK] - first
            oh = jnp.where(it == rel, 1.0, 0.0).astype(jnp.bfloat16)
            acc = acc + jnp.dot(oh, val_ref[k * BK:(k + 1) * BK, :], preferred_element_type=jnp.float32)
        out_ref[pl.ds(pl.multiple_of(first, BR), BR), :] = acc
        return 0
    lax.fori_loop(0, rows // BR, blk, 0)

def settle(idx, val, rows, BR=256, BK=512):
    return pl.pallas_call(functools.partial(settle_kernel, BR, BK), out_shape=jax.ShapeDtypeStruct((rows,128), jnp.float32),
        in_specs=[V, V], out_specs=V, compiler_params=BIG, name="settle")(idx.reshape(1,-1), val)

def rmw_kernel(NB, CH, idx_ref, val_ref, out_ref, *banks):
    n = val_ref.shape[0]
    per = n // NB
    stage = banks[-NB:]
    accs = (out_ref,) + tuple(banks[:NB - 1])
    for a in accs:
        a[...] = jnp.zeros_like(a)
    def chunk(c, _):
        for k in range(NB):
            base = k * per + c * CH
            stage[k][...] = val_ref[pl.ds(pl.multiple_of(base, CH), CH), :].astype(jnp.float32)
        for j in range(CH):
            ix = [idx_ref[k * per + c * CH + j] for k in range(NB)]
            new = [accs[k][pl.ds(ix[k], 1), :] + stage[k][pl.ds(j, 1), :] for k in range(NB)]
            for k in range(NB):
                accs[k][pl.ds(ix[k], 1), :] = new[k]
        return 0
    lax.fori_loop(0, per // CH, chunk, 0)
    if NB > 1:
        tot = out_ref[...]
        for a in accs[1:]:
            tot = tot + a[...]
        out_ref[...] = tot

def rmw(idx, val, rows, NB=4, CH=16):
    return pl.pallas_call(functools.partial(rmw_kernel, NB, CH), out_shape=jax.ShapeDtypeStruct((rows,128), jnp.float32),
        in_specs=[S, V], out_specs=V, scratch_shapes=[pltpu.VMEM((rows,128), jnp.float32)]*(NB-1)+[pltpu.VMEM((CH,128), jnp.float32)]*NB,
        compiler_params=BIG, name="settle_rows")(idx, val)

def mlp_kernel(hpos, cpos, hrow, crow, bottom, labels, w1_hbm, w2_hbm, wo, hsend, csend, w1, w2, h32, c32, x, g32, sem):
    cp1 = pltpu.make_async_copy(w1_hbm, w1, sem.at[0])
    cp2 = pltpu.make_async_copy(w2_hbm, w2, sem.at[1])
    cp1.start()
    cp2.start()
    h32[...] = hrow[...].astype(jnp.float32)
    c32[...] = crow[...].astype(jnp.float32)
    UN = 16
    for f in range(8):
        def body(k, _):
            for j in range(UN):
                b = k * UN + j
                v = h32[pl.ds(hpos[2 * f, b], 1), :] + h32[pl.ds(hpos[2 * f + 1, b], 1), :] + c32[pl.ds(cpos[f, b], 1), :]
                g32[f, pl.ds(b, 1), :] = v
            return 0
        lax.fori_loop(0, 128 // UN, body, 0)
    x[:, :128] = bottom[...]
    for f in range(8):
        x[:, (f + 1) * 128:(f + 2) * 128] = g32[f].astype(jnp.bfloat16)
    h32[...] = jnp.zeros_like(h32)
    c32[...] = jnp.zeros_like(c32)
    cp1.wait()
    p1 = jnp.dot(x[...], w1[...], preferred_element_type=jnp.float32)
    a1 = jnp.maximum(p1, 0.0).astype(jnp.bfloat16)
    cp2.wait()
    p2 = jnp.dot(a1, w2[...], preferred_element_type=jnp.float32)
    a2 = jnp.maximum(p2, 0.0).astype(jnp.bfloat16)
    wof = wo[...].astype(jnp.float32)
    score = jnp.sum(a2.astype(jnp.float32) * wof, axis=1, keepdims=True)
    delta = jax.nn.sigmoid(score) - labels[...]
    g2 = jnp.where(p2 > 0, delta * wof, 0.0).astype(jnp.bfloat16)
    NT = (((1,), (1,)), ((), ()))
    b2 = lax.dot_general(g2, w2[...], NT, preferred_element_type=jnp.float32)
    g1 = jnp.where(a1 > 0, b2, 0.0).astype(jnp.bfloat16)
    for f in range(8):
        g32[f] = lax.dot_general(g1, w1[(f + 1) * 128:(f + 2) * 128, :], NT, preferred_element_type=jnp.float32)
    for f in range(8):
        def body2(k, _):
            for j in range(UN):
                b = k * UN + j
                v = g32[f, pl.ds(b, 1), :]
                h32[pl.ds(hpos[2 * f, b], 1), :] = v
                h32[pl.ds(hpos[2 * f + 1, b], 1), :] = v
                c32[pl.ds(cpos[f, b], 1), :] = v
            return 0
        lax.fori_loop(0, 128 // UN, body2, 0)
    hsend[...] = h32[...].astype(jnp.bfloat16)
    csend[...] = c32[...].astype(jnp.bfloat16)

ANY = pl.BlockSpec(memory_space=pl.ANY)
def mlp(hpos, cpos, hrow, crow, bottom, labels, w1, w2, wo):
    sh = jax.ShapeDtypeStruct((4096,128), jnp.bfloat16)
    return pl.pallas_call(mlp_kernel, out_shape=[sh, sh], in_specs=[S,S,V,V,V,V,ANY,ANY,V], out_specs=[V,V],
        scratch_shapes=[pltpu.VMEM((1152,2048), jnp.bfloat16), pltpu.VMEM((2048,2048), jnp.bfloat16),
          pltpu.VMEM((4096,128), jnp.float32), pltpu.VMEM((4096,128), jnp.float32), pltpu.VMEM((128,1152), jnp.bfloat16),
          pltpu.VMEM((8,128,128), jnp.float32), pltpu.SemaphoreType.DMA((2,))], compiler_params=BIG, name="mlp")(hpos,cpos,hrow,crow,bottom,labels,w1,w2,wo)


STEP_RATE = 0.5


def update(embedding, accum, gradient):
    new_accum = accum + jnp.mean(gradient * gradient, axis=1)
    return (embedding - STEP_RATE * gradient / jnp.sqrt(new_accum)[:, None], new_accum)


def shards(hot_table, hot_acc, cold_table, cold_acc, bottom_out, labels, hot_owner, hot_offset,
           cold_owner, cold_offset, w_first, w_second, w_out):
    def flat(x):
        return jnp.transpose(x, (1, 2, 0)).reshape(-1, 128)
    hreq, hpos, creq, cpos = place(flat(hot_owner), flat(hot_offset), flat(cold_owner), flat(cold_offset))
    def swap(x, axes):
        return lax.all_to_all(x, axes, split_axis=0, concat_axis=0, tiled=True)
    both = ("group", "member")
    hask = swap(hreq.reshape(16, 1, 256), "member").reshape(-1)
    cask = swap(creq.reshape(128, 1, 32), both).reshape(-1)
    hrow = swap(serve(hask, hot_table).reshape(16, 256, 128), "member").reshape(-1, 128)
    crow = swap(serve(cask, cold_table).reshape(128, 32, 128), both).reshape(-1, 128)
    hsend, csend = mlp(hpos, cpos, hrow, crow, bottom_out, labels.reshape(128, 1), w_first, w_second, w_out.reshape(1, -1))
    hgot = swap(hsend.reshape(16, 256, 128), "member").reshape(-1, 128)
    hot_part = settle(hask, hgot, 2048, 512, 1024)
    mine = swap(hot_part.astype(jnp.bfloat16).reshape(8, 256, 128), "group")
    total = jnp.sum(mine.astype(jnp.float32), axis=0).astype(jnp.bfloat16)
    hot_grad = swap(jnp.broadcast_to(total[None], (8, 256, 128)), "group").reshape(2048, 128).astype(jnp.float32)
    cgot = swap(csend.reshape(128, 32, 128), both).reshape(-1, 128)
    cold_grad = rmw(cask, cgot, 4096)
    new_hot, new_hot_acc = update(hot_table, hot_acc, hot_grad)
    new_cold, new_cold_acc = update(cold_table, cold_acc, cold_grad)
    return (new_hot, new_hot_acc, new_cold, new_cold_acc)


def solution(mesh):
    both = P(("group", "member"))
    in_specs = (P("member"), P("member")) + (both,) * 8 + (P(),) * 3
    out_specs = (P("member"), P("member"), both, both)
    return jax.shard_map(shards, mesh=mesh, in_specs=in_specs, out_specs=out_specs, check_vma=False)
```

```python
import functools

import jax
import jax.numpy as jnp
from jax import lax
from jax.experimental import pallas as pl
from jax.experimental.pallas import tpu as pltpu
from jax.sharding import PartitionSpec as P

STEP_RATE = 0.5
LANES = 128
MEMBERS = 16
GROUPS = 8
DEVICES = 128
HOT_ROWS = 2048
COLD_ROWS = 4096
HCAP = 256
CCAP = 32
HIDDEN = 2048
TABLES = 8
SLICE = HOT_ROWS // GROUPS
MESH = pl.DeviceIdType.MESH
NT = (((1,), (1,)), ((), ()))

VMEM = pl.BlockSpec(memory_space=pltpu.VMEM)
SMEM = pl.BlockSpec(memory_space=pltpu.SMEM)
ANY = pl.BlockSpec(memory_space=pl.ANY)
DMA = pltpu.SemaphoreType.DMA


def f32(*shape):
    return pltpu.VMEM(shape, jnp.float32)


def b16(*shape):
    return pltpu.VMEM(shape, jnp.bfloat16)


def peer(step):
    group, member = lax.axis_index("group"), lax.axis_index("member")
    dx, dz, dc, dy = step % 4, (step // 4) % 4, (step // 16) % 2, step // 32
    to_group = (group // 2 + dy) % 4 * 2 + (group % 2 + dc) % 2
    to_member = (member // 4 + dz) % 4 * 4 + (member % 4 + dx) % 4
    return to_group, to_member


def greet_all():
    barrier = pltpu.get_barrier_semaphore()

    def signal(step, unused):
        pl.semaphore_signal(barrier, inc=1, device_id=peer(step), device_id_type=MESH)
        return unused

    lax.fori_loop(1, DEVICES, signal, 0)
    return barrier


def mixed(step):
    return step * 45 % DEVICES


def remote(src, dst, send, recv, to):
    return pltpu.make_async_remote_copy(
        src_ref=src, dst_ref=dst, send_sem=send, recv_sem=recv, device_id=to, device_id_type=MESH
    )


def place(owner_ref, offset_ref, owners, cap, request_ref, position_ref):
    rows = owner_ref.shape[0]
    owner_ids = lax.broadcasted_iota(jnp.int32, (owners, LANES), 0)
    hits = [(owner_ref[r : r + 1, :] == owner_ids).astype(jnp.float32) for r in range(rows)]
    stacked = jnp.concatenate(hits, axis=0).astype(jnp.bfloat16)
    first = lax.broadcasted_iota(jnp.int32, (LANES, LANES), 0)
    second = lax.broadcasted_iota(jnp.int32, (LANES, LANES), 1)
    earlier = (first < second).astype(jnp.float32)
    side = jnp.concatenate([earlier, jnp.ones((LANES, LANES), jnp.float32)], axis=1)
    counts = jnp.dot(stacked, side.astype(jnp.bfloat16), preferred_element_type=jnp.float32)
    base = jnp.zeros((owners, LANES), jnp.float32)
    slots = lax.broadcasted_iota(jnp.int32, (cap, LANES), 0)
    high, low, at_slot = [], [], []
    for r in range(rows):
        count = counts[r * owners : (r + 1) * owners]
        slot = jnp.sum(hits[r] * (count[:, :LANES] + base), axis=0, keepdims=True).astype(jnp.int32)
        base = base + count[:, LANES:]
        position_ref[r : r + 1, :] = owner_ref[r : r + 1, :] * cap + slot
        offset = offset_ref[r : r + 1, :]
        high.append(hits[r] * (offset // 64).astype(jnp.float32))
        low.append(hits[r] * (offset % 64).astype(jnp.float32))
        at_slot.append((slots == slot).astype(jnp.float32).astype(jnp.bfloat16))
    digits = jnp.concatenate(
        [jnp.concatenate(high, axis=1), jnp.concatenate(low, axis=1)], axis=0
    ).astype(jnp.bfloat16)
    placed = lax.dot_general(
        digits, jnp.concatenate(at_slot, axis=1), NT, preferred_element_type=jnp.float32
    )
    requests = (placed[:owners] * 64.0 + placed[owners:]).astype(jnp.int32)
    for owner in range(owners):
        request_ref[owner, :, :cap] = requests[owner : owner + 1, :]


def place_kernel(
    hot_owner, hot_offset, cold_owner, cold_offset, hot_request, hot_pos, cold_request, cold_pos
):
    cold_request[...] = jnp.zeros_like(cold_request)
    place(hot_owner, hot_offset, MEMBERS, HCAP, hot_request, hot_pos)
    place(cold_owner, cold_offset, DEVICES, CCAP, cold_request, cold_pos)


def place_all(hot_owner, hot_offset, cold_owner, cold_offset):
    shapes = [
        (MEMBERS, 1, HCAP), (2 * TABLES, LANES), (DEVICES, 1, LANES), (TABLES, LANES)
    ]
    return pl.pallas_call(
        place_kernel,
        out_shape=[jax.ShapeDtypeStruct(shape, jnp.int32) for shape in shapes],
        in_specs=[VMEM] * 4,
        out_specs=[VMEM] * 4,
        compiler_params=pltpu.CompilerParams(vmem_limit_bytes=32 << 20),
        name="place",
    )(hot_owner, hot_offset, cold_owner, cold_offset)


def fetch_kernel(
    hot_request, cold_request, hot_hbm, cold_hbm,
    hot_asked, cold_asked, hot_rows, cold_rows,
    hot_table, cold_table, hot_index, cold_index,
    hot_out, cold_out, stage, local_sem, send_sem, recv_sem,
):
    group, member = lax.axis_index("group"), lax.axis_index("member")
    me = group * MEMBERS + member
    barrier = greet_all()
    hot_load = pltpu.make_async_copy(hot_hbm, hot_table, local_sem.at[0])
    cold_load = pltpu.make_async_copy(cold_hbm, cold_table, local_sem.at[1])
    hot_load.start()
    cold_load.start()
    pl.semaphore_wait(barrier, DEVICES - 1)

    def ask_hot(step, unused):
        to = peer(step)
        remote(hot_request.at[to[1]], hot_asked.at[member], send_sem.at[0], recv_sem.at[0], to).start()
        return unused

    def ask_cold(step, unused):
        to = peer(mixed(step))
        remote(
            cold_request.at[to[0] * MEMBERS + to[1]], cold_asked.at[me],
            send_sem.at[1], recv_sem.at[1], to,
        ).start()
        return unused

    lax.fori_loop(1, MEMBERS, ask_hot, 0)
    lax.fori_loop(1, DEVICES, ask_cold, 0)
    hot_asked[member] = hot_request[member]
    cold_asked[me] = cold_request[me]

    next_peer = peer(1)

    def drain(buffer, parts, which):
        part = buffer.at[pl.ds(0, parts)]
        return remote(part, part, send_sem.at[which], recv_sem.at[which], next_peer)

    drain(hot_asked, MEMBERS - 1, 0).wait_recv()
    to_scalars = pltpu.make_async_copy(hot_asked, hot_index, local_sem.at[2])
    to_scalars.start()
    hot_load.wait()
    to_scalars.wait()

    def pick(table, index, owner, first, target):
        for j in range(CCAP):
            stage[pl.ds(j, 1), :] = table[pl.ds(index[owner, 0, first + j], 1), :]
        target[...] = stage[...].astype(jnp.bfloat16)

    def serve_hot(step, unused):
        to = peer(step)

        def chunk(c, carry):
            first = pl.multiple_of(c * CCAP, CCAP)
            pick(hot_table, hot_index, to[1], first, hot_out.at[to[1], pl.ds(first, CCAP), :])
            return carry

        lax.fori_loop(0, HCAP // CCAP, chunk, 0)
        return unused

    def serve_hot_send(step, unused):
        serve_hot(step, unused)
        to = peer(step)
        remote(hot_out.at[to[1]], hot_rows.at[member], send_sem.at[2], recv_sem.at[2], to).start()
        return unused

    lax.fori_loop(1, MEMBERS, serve_hot_send, 0)
    serve_hot(0, 0)
    hot_rows[member] = hot_out[member]

    drain(cold_asked, DEVICES - 1, 1).wait_recv()
    to_scalars = pltpu.make_async_copy(cold_asked, cold_index, local_sem.at[3])
    to_scalars.start()
    cold_load.wait()
    to_scalars.wait()

    def serve_cold_send(step, unused):
        to = peer(mixed(step))
        device = to[0] * MEMBERS + to[1]
        pick(cold_table, cold_index, device, 0, cold_out.at[device])
        remote(cold_out.at[device], cold_rows.at[me], send_sem.at[3], recv_sem.at[3], to).start()
        return unused

    lax.fori_loop(1, DEVICES, serve_cold_send, 0)
    pick(cold_table, cold_index, me, 0, cold_rows.at[me])

    drain(hot_request, MEMBERS - 1, 0).wait_send()
    drain(cold_request, DEVICES - 1, 1).wait_send()
    drain(hot_rows, MEMBERS - 1, 2).wait()
    drain(cold_rows, DEVICES - 1, 3).wait()


def fetch(hot_request, cold_request, hot_table, cold_table):
    i32 = jnp.int32
    shape = jax.ShapeDtypeStruct
    return pl.pallas_call(
        fetch_kernel,
        out_shape=[
            shape((MEMBERS, 1, HCAP), i32), shape((DEVICES, 1, LANES), i32),
            shape((MEMBERS, HCAP, LANES), jnp.bfloat16), shape((DEVICES, CCAP, LANES), jnp.bfloat16),
        ],
        in_specs=[VMEM] * 2 + [ANY] * 2,
        out_specs=[VMEM] * 4,
        scratch_shapes=[
            f32(HOT_ROWS, LANES), f32(COLD_ROWS, LANES),
            pltpu.SMEM((MEMBERS, 1, HCAP), i32), pltpu.SMEM((DEVICES, 1, LANES), i32),
            b16(MEMBERS, HCAP, LANES), b16(DEVICES, CCAP, LANES), f32(CCAP, LANES),
            DMA((4,)), DMA((4,)), DMA((4,)),
        ],
        compiler_params=pltpu.CompilerParams(
            collective_id=0, has_side_effects=True, vmem_limit_bytes=40 << 20
        ),
        name="fetch",
    )(hot_request, cold_request, hot_table, cold_table)


def network_kernel(
    hot_pos, cold_pos, hot_rows, cold_rows, bottom, labels, first_hbm, second_hbm, w_out,
    hot_send, cold_send,
    w_first, w_second, hot_wide, cold_wide, features, pooled, sem,
):
    load_first = pltpu.make_async_copy(first_hbm, w_first, sem.at[0])
    load_second = pltpu.make_async_copy(second_hbm, w_second, sem.at[1])
    load_first.start()
    load_second.start()
    hot_wide[...] = hot_rows[...].astype(jnp.float32)
    cold_wide[...] = cold_rows[...].astype(jnp.float32)
    unroll = 16
    for table in range(TABLES):

        def combine(k, unused):
            for j in range(unroll):
                b = k * unroll + j
                hot = (
                    hot_wide[pl.ds(hot_pos[2 * table, b], 1), :]
                    + hot_wide[pl.ds(hot_pos[2 * table + 1, b], 1), :]
                )
                pooled[table, pl.ds(b, 1), :] = hot + cold_wide[pl.ds(cold_pos[table, b], 1), :]
            return unused

        lax.fori_loop(0, LANES // unroll, combine, 0)
    features[:, :LANES] = bottom[...]
    for table in range(TABLES):
        features[:, (table + 1) * LANES : (table + 2) * LANES] = pooled[table].astype(jnp.bfloat16)
    hot_wide[...] = jnp.zeros_like(hot_wide)
    cold_wide[...] = jnp.zeros_like(cold_wide)
    load_first.wait()
    first_pre = jnp.dot(features[...], w_first[...], preferred_element_type=jnp.float32)
    first_act = jnp.maximum(first_pre, 0.0).astype(jnp.bfloat16)
    load_second.wait()
    second_pre = jnp.dot(first_act, w_second[...], preferred_element_type=jnp.float32)
    second_act = jnp.maximum(second_pre, 0.0).astype(jnp.bfloat16)
    out_wide = w_out[...].astype(jnp.float32)
    score = jnp.sum(second_act.astype(jnp.float32) * out_wide, axis=1, keepdims=True)
    delta = jax.nn.sigmoid(score) - labels[...]
    grad_second = jnp.where(second_pre > 0, delta * out_wide, 0.0).astype(jnp.bfloat16)
    back_second = lax.dot_general(grad_second, w_second[...], NT, preferred_element_type=jnp.float32)
    grad_first = jnp.where(first_pre > 0, back_second, 0.0).astype(jnp.bfloat16)
    for table in range(TABLES):
        pooled[table] = lax.dot_general(
            grad_first, w_first[(table + 1) * LANES : (table + 2) * LANES, :], NT,
            preferred_element_type=jnp.float32,
        )
    for table in range(TABLES):

        def spread(k, unused):
            for j in range(unroll):
                b = k * unroll + j
                term = pooled[table, pl.ds(b, 1), :]
                hot_wide[pl.ds(hot_pos[2 * table, b], 1), :] = term
                hot_wide[pl.ds(hot_pos[2 * table + 1, b], 1), :] = term
                cold_wide[pl.ds(cold_pos[table, b], 1), :] = term
            return unused

        lax.fori_loop(0, LANES // unroll, spread, 0)
    hot_send[...] = hot_wide[...].astype(jnp.bfloat16)
    cold_send[...] = cold_wide[...].astype(jnp.bfloat16)


def network(hot_pos, cold_pos, hot_rows, cold_rows, bottom, labels, w_first, w_second, w_out):
    return pl.pallas_call(
        network_kernel,
        out_shape=[
            jax.ShapeDtypeStruct(hot_rows.shape, jnp.bfloat16),
            jax.ShapeDtypeStruct(cold_rows.shape, jnp.bfloat16),
        ],
        in_specs=[SMEM, SMEM, VMEM, VMEM, VMEM, VMEM, ANY, ANY, VMEM],
        out_specs=[VMEM, VMEM],
        scratch_shapes=[
            b16(*w_first.shape), b16(*w_second.shape), f32(*hot_rows.shape), f32(*cold_rows.shape),
            b16(LANES, w_first.shape[0]), f32(TABLES, LANES, LANES), DMA((2,)),
        ],
        compiler_params=pltpu.CompilerParams(vmem_limit_bytes=48 << 20),
        name="network",
    )(hot_pos, cold_pos, hot_rows, cold_rows, bottom, labels, w_first, w_second, w_out)


def settle_kernel(
    hot_send, cold_send, hot_asked, cold_got, hot_grad,
    hot_got, partial, part_out, part_got, send_sem, recv_sem,
):
    group, member = lax.axis_index("group"), lax.axis_index("member")
    me = group * MEMBERS + member
    barrier = greet_all()
    pl.semaphore_wait(barrier, DEVICES - 1)
    half = MEMBERS // 2

    def send_hot(step, unused):
        to = peer(step)
        remote(
            hot_send.at[to[1]], hot_got.at[step], send_sem.at[0], recv_sem.at[0], to
        ).start()
        return unused

    def send_hot_late(step, unused):
        to = peer(step)
        remote(
            hot_send.at[to[1]], hot_got.at[step], send_sem.at[0], recv_sem.at[1], to
        ).start()
        return unused

    def send_cold(step, unused):
        to = peer(mixed(step))
        remote(
            cold_send.at[to[0] * MEMBERS + to[1]], cold_got.at[me], send_sem.at[1], recv_sem.at[2], to
        ).start()
        return unused

    lax.fori_loop(1, half, send_hot, 0)
    lax.fori_loop(half, MEMBERS, send_hot_late, 0)
    lax.fori_loop(1, DEVICES, send_cold, 0)
    hot_got[0] = hot_send[member]
    cold_got[me] = cold_send[me]
    next_peer = peer(1)

    def drain(buffer, first, parts, send, recv):
        part = buffer.at[pl.ds(first, parts)]
        return remote(part, part, send_sem.at[send], recv_sem.at[recv], next_peer)

    def source(step):
        return (member // 4 + 4 - step // 4) % 4 * 4 + (member % 4 + 4 - step % 4) % 4

    row_ids = lax.broadcasted_iota(jnp.int32, (SLICE, HCAP), 0)

    def add_up(first, steps, total):
        for step in steps:
            wanted = hot_asked[source(step)] - first
            chosen = jnp.where(row_ids == wanted, 1.0, 0.0).astype(jnp.bfloat16)
            total = total + jnp.dot(chosen, hot_got[step], preferred_element_type=jnp.float32)
        return total

    drain(hot_got, 1, half - 1, 0, 0).wait_recv()

    def early(block, unused):
        partial[block] = add_up(block * SLICE, range(half), jnp.zeros((SLICE, LANES), jnp.float32))
        return unused

    lax.fori_loop(0, GROUPS, early, 0)
    drain(hot_got, half, MEMBERS - half, 0, 1).wait_recv()

    def late(step, unused):
        to_group = (group // 2 + step // 2) % 4 * 2 + (group % 2 + step % 2) % 2
        total = add_up(to_group * SLICE, range(half, MEMBERS), partial[to_group])
        partial[to_group] = total
        part_out[to_group] = total.astype(jnp.bfloat16)
        return to_group

    def late_send(step, unused):
        to_group = late(step, unused)
        remote(
            part_out.at[to_group], part_got.at[step], send_sem.at[2], recv_sem.at[3],
            (to_group, member),
        ).start()
        return unused

    lax.fori_loop(1, GROUPS, late_send, 0)
    late(0, 0)
    drain(part_got, 1, GROUPS - 1, 2, 3).wait_recv()
    total = partial[group]
    for step in range(1, GROUPS):
        total = total + part_got[step].astype(jnp.float32)
    hot_grad[group] = total.astype(jnp.bfloat16)

    def share(step, unused):
        to_group = (group // 2 + step // 2) % 4 * 2 + (group % 2 + step % 2) % 2
        remote(
            hot_grad.at[group], hot_grad.at[group], send_sem.at[3], recv_sem.at[4],
            (to_group, member),
        ).start()
        return unused

    lax.fori_loop(1, GROUPS, share, 0)
    drain(hot_send, 0, MEMBERS - 1, 0, 0).wait_send()
    drain(cold_send, 0, DEVICES - 1, 1, 2).wait()
    drain(part_out, 0, GROUPS - 1, 2, 3).wait_send()
    drain(hot_grad, 0, GROUPS - 1, 3, 4).wait()


def settle(hot_send, cold_send, hot_asked):
    return pl.pallas_call(
        settle_kernel,
        out_shape=[
            jax.ShapeDtypeStruct(cold_send.shape, jnp.bfloat16),
            jax.ShapeDtypeStruct((GROUPS, SLICE, LANES), jnp.bfloat16),
        ],
        in_specs=[VMEM] * 3,
        out_specs=[VMEM] * 2,
        scratch_shapes=[
            b16(*hot_send.shape), f32(GROUPS, SLICE, LANES), b16(GROUPS, SLICE, LANES),
            b16(GROUPS, SLICE, LANES), DMA((4,)), DMA((5,)),
        ],
        compiler_params=pltpu.CompilerParams(
            collective_id=1, has_side_effects=True, vmem_limit_bytes=40 << 20
        ),
        name="settle",
    )(hot_send, cold_send, hot_asked)


BANKS = 4


def update_kernel(
    cold_index, cold_got, hot_grad, hot_acc, cold_acc, hot_hbm, cold_hbm,
    new_hot_hbm, new_hot_acc, new_cold_hbm, new_cold_acc,
    hot_table, cold_table, new_hot, new_cold, *rest,
):
    banks, stages, sem = rest[:BANKS], rest[BANKS : 2 * BANKS], rest[2 * BANKS]
    load_hot = pltpu.make_async_copy(hot_hbm, hot_table, sem.at[0])
    load_cold = pltpu.make_async_copy(cold_hbm, cold_table, sem.at[1])
    load_hot.start()
    load_cold.start()
    first = lax.broadcasted_iota(jnp.int32, (LANES, LANES), 0)
    second = lax.broadcasted_iota(jnp.int32, (LANES, LANES), 1)
    diagonal = first == second

    def step(block, table, acc, new_table, new_acc, gradient):
        rows = pl.ds(pl.multiple_of(block * LANES, LANES), LANES)
        spread_acc = jnp.where(diagonal, acc[pl.ds(block, 1), :], 0.0)
        new = jnp.sum(gradient * gradient * (1.0 / LANES) + spread_acc, axis=1, keepdims=True)
        new_table[rows, :] = table[rows, :] - STEP_RATE * gradient * lax.rsqrt(new)
        new_acc[pl.ds(block, 1), :] = jnp.sum(jnp.where(diagonal, new, 0.0), axis=0, keepdims=True)

    load_hot.wait()

    def hot_block(block, unused):
        slice_rows = pl.ds(pl.multiple_of(block % 2 * LANES, LANES), LANES)
        gradient = hot_grad[block // 2, slice_rows, :].astype(jnp.float32)
        step(block, hot_table, hot_acc, new_hot, new_hot_acc, gradient)
        return unused

    lax.fori_loop(0, HOT_ROWS // LANES, hot_block, 0)
    store_hot = pltpu.make_async_copy(new_hot, new_hot_hbm, sem.at[2])
    store_hot.start()

    for bank in banks:
        bank[...] = jnp.zeros_like(bank)
    per_bank = DEVICES // BANKS

    def add_rows(c, unused):
        for k in range(BANKS):
            stages[k][...] = cold_got[k * per_bank + c].astype(jnp.float32)
        for j in range(CCAP):
            at = [cold_index[k * per_bank + c, 0, j] for k in range(BANKS)]
            new = [banks[k][pl.ds(at[k], 1), :] + stages[k][pl.ds(j, 1), :] for k in range(BANKS)]
            for k in range(BANKS):
                banks[k][pl.ds(at[k], 1), :] = new[k]
        return unused

    lax.fori_loop(0, per_bank, add_rows, 0)
    load_cold.wait()

    def cold_block(block, unused):
        rows = pl.ds(pl.multiple_of(block * LANES, LANES), LANES)
        gradient = banks[0][rows, :]
        for bank in banks[1:]:
            gradient = gradient + bank[rows, :]
        step(block, cold_table, cold_acc, new_cold, new_cold_acc, gradient)
        return unused

    lax.fori_loop(0, COLD_ROWS // LANES, cold_block, 0)
    store_cold = pltpu.make_async_copy(new_cold, new_cold_hbm, sem.at[3])
    store_cold.start()
    store_hot.wait()
    store_cold.wait()


def update(cold_index, cold_got, hot_grad, hot_acc, cold_acc, hot_table, cold_table):
    shape = jax.ShapeDtypeStruct
    return pl.pallas_call(
        update_kernel,
        out_shape=[
            shape(hot_table.shape, jnp.float32), shape(hot_acc.shape, jnp.float32),
            shape(cold_table.shape, jnp.float32), shape(cold_acc.shape, jnp.float32),
        ],
        in_specs=[SMEM] + [VMEM] * 4 + [ANY] * 2,
        out_specs=[ANY, VMEM, ANY, VMEM],
        scratch_shapes=[
            f32(HOT_ROWS, LANES), f32(COLD_ROWS, LANES), f32(HOT_ROWS, LANES), f32(COLD_ROWS, LANES),
        ] + [f32(COLD_ROWS, LANES)] * BANKS + [f32(CCAP, LANES)] * BANKS + [DMA((4,))],
        compiler_params=pltpu.CompilerParams(vmem_limit_bytes=48 << 20),
        name="update",
    )(cold_index, cold_got, hot_grad, hot_acc, cold_acc, hot_table, cold_table)


def shards(
    hot_table, hot_acc, cold_table, cold_acc, bottom_out, labels,
    hot_owner, hot_offset, cold_owner, cold_offset, w_first, w_second, w_out,
):
    def by_lane(lookups):
        return jnp.transpose(lookups, (1, 2, 0)).reshape(-1, LANES)

    hot_request, hot_pos, cold_request, cold_pos = place_all(
        by_lane(hot_owner), by_lane(hot_offset), by_lane(cold_owner), by_lane(cold_offset)
    )
    hot_asked, cold_asked, hot_rows, cold_rows = fetch(
        hot_request, cold_request, hot_table, cold_table
    )
    hot_send, cold_send = network(
        hot_pos, cold_pos, hot_rows.reshape(-1, LANES), cold_rows.reshape(-1, LANES), bottom_out,
        labels.reshape(-1, 1), w_first, w_second, w_out.reshape(1, -1),
    )
    cold_got, hot_grad = settle(
        hot_send.reshape(MEMBERS, HCAP, LANES), cold_send.reshape(DEVICES, CCAP, LANES), hot_asked
    )
    new_hot, new_hot_acc, new_cold, new_cold_acc = update(
        cold_asked, cold_got, hot_grad, hot_acc.reshape(-1, LANES), cold_acc.reshape(-1, LANES),
        hot_table, cold_table,
    )
    return (new_hot, new_hot_acc.reshape(-1), new_cold, new_cold_acc.reshape(-1))


def solution(mesh):
    both = P(("group", "member"))
    in_specs = (P("member"), P("member")) + (both,) * 8 + (P(),) * 3
    out_specs = (P("member"), P("member"), both, both)
    return jax.shard_map(shards, mesh=mesh, in_specs=in_specs, out_specs=out_specs, check_vma=False)
```

```python
import functools

import jax
import jax.numpy as jnp
from jax import lax
from jax.experimental import pallas as pl
from jax.experimental.pallas import tpu as pltpu
from jax.sharding import PartitionSpec as P

STEP_RATE = 0.5
LANES = 128
MEMBERS = 16
GROUPS = 8
DEVICES = 128
HOT_ROWS = 2048
COLD_ROWS = 4096
HCAP = 256
CCAP = 32
HIDDEN = 2048
TABLES = 8
SLICE = HOT_ROWS // GROUPS
MESH = pl.DeviceIdType.MESH
NT = (((1,), (1,)), ((), ()))

VMEM = pl.BlockSpec(memory_space=pltpu.VMEM)
ANY = pl.BlockSpec(memory_space=pl.ANY)
DMA = pltpu.SemaphoreType.DMA


def f32(*shape):
    return pltpu.VMEM(shape, jnp.float32)


def b16(*shape):
    return pltpu.VMEM(shape, jnp.bfloat16)


def remote(src, dst, send, recv, to):
    return pltpu.make_async_remote_copy(
        src_ref=src, dst_ref=dst, send_sem=send, recv_sem=recv, device_id=to, device_id_type=MESH
    )


def place(owner_ref, offset_ref, owners, cap, request_ref, position_ref):
    rows = owner_ref.shape[0]
    owner_ids = lax.broadcasted_iota(jnp.int32, (owners, LANES), 0)
    hits = [(owner_ref[r : r + 1, :] == owner_ids).astype(jnp.float32) for r in range(rows)]
    stacked = jnp.concatenate(hits, axis=0).astype(jnp.bfloat16)
    first = lax.broadcasted_iota(jnp.int32, (LANES, LANES), 0)
    second = lax.broadcasted_iota(jnp.int32, (LANES, LANES), 1)
    earlier = (first < second).astype(jnp.float32)
    side = jnp.concatenate([earlier, jnp.ones((LANES, LANES), jnp.float32)], axis=1)
    counts = jnp.dot(stacked, side.astype(jnp.bfloat16), preferred_element_type=jnp.float32)
    base = jnp.zeros((owners, LANES), jnp.float32)
    width = request_ref.shape[2]
    slots = lax.broadcasted_iota(jnp.int32, (width, LANES), 0) % cap
    high, low, at_slot = [], [], []
    for r in range(rows):
        count = counts[r * owners : (r + 1) * owners]
        slot = jnp.sum(hits[r] * (count[:, :LANES] + base), axis=0, keepdims=True).astype(jnp.int32)
        base = base + count[:, LANES:]
        position_ref[r : r + 1, :] = owner_ref[r : r + 1, :] * cap + slot
        offset = offset_ref[r : r + 1, :]
        high.append(hits[r] * (offset // 64).astype(jnp.float32))
        low.append(hits[r] * (offset % 64).astype(jnp.float32))
        at_slot.append((slots == slot).astype(jnp.float32).astype(jnp.bfloat16))
    digits = jnp.concatenate(
        [jnp.concatenate(high, axis=1), jnp.concatenate(low, axis=1)], axis=0
    ).astype(jnp.bfloat16)
    placed = lax.dot_general(
        digits, jnp.concatenate(at_slot, axis=1), NT, preferred_element_type=jnp.float32
    )
    requests = (placed[:owners] * 64.0 + placed[owners:]).astype(jnp.int32)
    for owner in range(owners):
        request_ref[owner] = requests[owner : owner + 1, :]


def place_kernel(
    hot_owner, hot_offset, cold_owner, cold_offset, hot_request, hot_pos, cold_request, cold_pos
):
    place(hot_owner, hot_offset, MEMBERS, HCAP, hot_request, hot_pos)
    place(cold_owner, cold_offset, DEVICES, CCAP, cold_request, cold_pos)


def place_all(hot_owner, hot_offset, cold_owner, cold_offset):
    shapes = [
        (MEMBERS, 1, HCAP), (2 * TABLES, LANES), (DEVICES, 1, LANES), (TABLES, LANES)
    ]
    return pl.pallas_call(
        place_kernel,
        out_shape=[jax.ShapeDtypeStruct(shape, jnp.int32) for shape in shapes],
        in_specs=[VMEM] * 4,
        out_specs=[VMEM] * 4,
        compiler_params=pltpu.CompilerParams(vmem_limit_bytes=32 << 20),
        name="place",
    )(hot_owner, hot_offset, cold_owner, cold_offset)


WAVES = 8
PAIRS = TABLES * LANES


def step_kernel(
    hot_request, cold_request, hot_pos, cold_pos, bottom, labels, w_out,
    hot_hbm, cold_hbm, first_hbm, second_hbm,
    hot_grad, cold_grad,
    hot_table, cold_table, w_first, w_second,
    hot_asked, cold_asked, hot_index, cold_index, hot_at, cold_at,
    hot_out, cold_out, hot_rows, cold_rows, stage, hot_wide, cold_wide, features, pooled, terms,
    hot_send, cold_send, hot_got, cold_got, partial, part_out, part_got,
    local_sem, send_sem, recv_sem, cold_sem,
):
    group, member = lax.axis_index("group"), lax.axis_index("member")
    me = group * MEMBERS + member
    z, x, y, core = lax.div(member, 4), lax.rem(member, 4), lax.div(group, 2), lax.rem(group, 2)
    xs = [lax.rem(x + d, 4) for d in range(4)]
    zs = [lax.rem(z + d, 4) * 4 for d in range(4)]
    members = [zs[d // 4] + xs[d % 4] for d in range(MEMBERS)]
    ys = [lax.rem(y + d, 4) * 2 for d in range(4)]
    cores = [core, 1 - core]
    to_group = [ys[k // 2] + cores[k % 2] for k in range(GROUPS)]
    from_group = [ys[(4 - k // 2) % 4] + cores[k % 2] for k in range(GROUPS)]

    def member_step(i):
        step = lax.rem(i * 7, MEMBERS)
        return lax.div(step, 4), lax.rem(step, 4)

    def to_member(i):
        dz, dx = member_step(i)
        return lax.rem(z + dz, 4) * 4 + lax.rem(x + dx, 4)

    def from_member(i):
        dz, dx = member_step(i)
        return lax.rem(z + 4 - dz, 4) * 4 + lax.rem(x + 4 - dx, 4)

    barrier = pltpu.get_barrier_semaphore()
    for k in range(GROUPS):
        for d in range(MEMBERS):
            if k or d:
                pl.semaphore_signal(
                    barrier, inc=1, device_id=(to_group[k], members[d]), device_id_type=MESH
                )
    loads = [
        pltpu.make_async_copy(src, dst, local_sem.at[n])
        for n, (src, dst) in enumerate(
            [
                (hot_hbm, hot_table), (cold_hbm, cold_table), (first_hbm, w_first),
                (second_hbm, w_second), (hot_pos, hot_at), (cold_pos, cold_at),
            ]
        )
    ]
    for load in loads:
        load.start()
    pl.semaphore_wait(barrier, DEVICES - 1)

    beside = (group, members[1])

    def drain(buffer, first, parts, send, recv):
        part = buffer.at[pl.ds(first, parts)]
        return remote(part, part, send, recv, beside)

    def ask_hot(i, unused):
        to = to_member(i)
        remote(
            hot_request.at[to], hot_asked.at[i], send_sem.at[0], recv_sem.at[0], (group, to)
        ).start()
        return unused

    lax.fori_loop(1, MEMBERS, ask_hot, 0)

    def ask_cold_at(i, groups):
        to = to_member(i)
        for k in groups:
            remote(
                cold_request.at[to_group[k] * MEMBERS + to], cold_asked.at[i * GROUPS + k],
                send_sem.at[1], recv_sem.at[1], (to_group[k], to),
            ).start()

    def ask_cold(i, unused):
        ask_cold_at(i, range(GROUPS))
        return unused

    ask_cold_at(0, range(1, GROUPS))
    lax.fori_loop(1, MEMBERS, ask_cold, 0)
    hot_asked[0] = hot_request[member]
    cold_asked[0] = cold_request[me]

    drain(hot_asked, 1, MEMBERS - 1, send_sem.at[0], recv_sem.at[0]).wait_recv()
    to_scalars = pltpu.make_async_copy(hot_asked, hot_index, local_sem.at[6])
    to_scalars.start()
    loads[0].wait()
    to_scalars.wait()

    def pick(table, index, row, first, target):
        for j in range(CCAP):
            stage[pl.ds(j, 1), :] = table[pl.ds(index[row, 0, first + j], 1), :]
        target[...] = stage[...].astype(jnp.bfloat16)

    def serve_hot(i, target):
        def chunk(c, unused):
            first = pl.multiple_of(c * CCAP, CCAP)
            pick(hot_table, hot_index, i, first, target.at[pl.ds(first, CCAP), :])
            return unused

        lax.fori_loop(0, HCAP // CCAP, chunk, 0)

    def serve_hot_send(i, unused):
        to = from_member(i)
        serve_hot(i, hot_out.at[i])
        remote(
            hot_out.at[i], hot_rows.at[member], send_sem.at[2], recv_sem.at[2], (group, to)
        ).start()
        return unused

    lax.fori_loop(1, MEMBERS, serve_hot_send, 0)
    serve_hot(0, hot_rows.at[member])

    drain(cold_asked, 1, DEVICES - 1, send_sem.at[1], recv_sem.at[1]).wait_recv()
    to_scalars = pltpu.make_async_copy(cold_asked, cold_index, local_sem.at[7])
    to_scalars.start()
    loads[1].wait()
    to_scalars.wait()

    def serve_cold_at(i, groups):
        to = from_member(i)
        for k in groups:
            n = i * GROUPS + k
            pick(cold_table, cold_index, n, 0, cold_out.at[n])
            remote(
                cold_out.at[n], cold_rows.at[me], send_sem.at[3], recv_sem.at[3],
                (from_group[k], to),
            ).start()

    def serve_cold(i, unused):
        serve_cold_at(i, range(GROUPS))
        return unused

    serve_cold_at(0, range(1, GROUPS))
    lax.fori_loop(1, MEMBERS, serve_cold, 0)
    pick(cold_table, cold_index, 0, 0, cold_rows.at[me])

    loads[4].wait()
    loads[5].wait()
    drain(hot_rows, 0, MEMBERS - 1, send_sem.at[2], recv_sem.at[2]).wait_recv()
    hot_wide[...] = hot_rows[...].astype(jnp.float32).reshape(hot_wide.shape)
    features[:, :LANES] = bottom[...]
    drain(cold_rows, 0, DEVICES - 1, send_sem.at[3], recv_sem.at[3]).wait_recv()
    cold_wide[...] = cold_rows[...].astype(jnp.float32).reshape(cold_wide.shape)
    unroll = 16
    for table in range(TABLES):

        def combine(k, unused):
            for j in range(unroll):
                b = k * unroll + j
                hot = (
                    hot_wide[pl.ds(hot_at[2 * table, b], 1), :]
                    + hot_wide[pl.ds(hot_at[2 * table + 1, b], 1), :]
                )
                pooled[table, pl.ds(b, 1), :] = hot + cold_wide[pl.ds(cold_at[table, b], 1), :]
            return unused

        lax.fori_loop(0, LANES // unroll, combine, 0)
        features[:, (table + 1) * LANES : (table + 2) * LANES] = pooled[table].astype(jnp.bfloat16)

    loads[2].wait()
    first_pre = jnp.dot(features[...], w_first[...], preferred_element_type=jnp.float32)
    first_act = jnp.maximum(first_pre, 0.0).astype(jnp.bfloat16)
    loads[3].wait()
    second_pre = jnp.dot(first_act, w_second[...], preferred_element_type=jnp.float32)
    second_act = jnp.maximum(second_pre, 0.0).astype(jnp.bfloat16)
    out_wide = w_out[...].astype(jnp.float32)
    score = jnp.sum(second_act.astype(jnp.float32) * out_wide, axis=1, keepdims=True)
    row_id = lax.broadcasted_iota(jnp.int32, (LANES, LANES), 0)
    lane_id = lax.broadcasted_iota(jnp.int32, (LANES, LANES), 1)
    label = jnp.sum(jnp.where(row_id == lane_id, labels[...], 0.0), axis=1, keepdims=True)
    delta = jax.nn.sigmoid(score) - label
    grad_second = jnp.where(second_pre > 0, delta * out_wide, 0.0).astype(jnp.bfloat16)
    back_second = lax.dot_general(grad_second, w_second[...], NT, preferred_element_type=jnp.float32)
    grad_first = jnp.where(first_pre > 0, back_second, 0.0).astype(jnp.bfloat16)
    for table in range(TABLES):
        terms[table * LANES : (table + 1) * LANES, :] = lax.dot_general(
            grad_first, w_first[(table + 1) * LANES : (table + 2) * LANES, :], NT,
            preferred_element_type=jnp.float32,
        ).astype(jnp.bfloat16)

    slot_id = lax.broadcasted_iota(jnp.int32, (HCAP, LANES), 0)

    def one_hot(rows, wanted):
        return jnp.concatenate([jnp.where(rows == w, 1.0, 0.0).astype(jnp.bfloat16) for w in wanted], axis=1)

    def spread_hot(to):
        base = to * HCAP
        wanted = []
        for table in range(TABLES):
            one = hot_pos[2 * table : 2 * table + 1, :] - base
            two = hot_pos[2 * table + 1 : 2 * table + 2, :] - base
            wanted.append(jnp.where((one >= 0) & (one < HCAP), one, two))
        return jnp.dot(
            one_hot(slot_id, wanted), terms[...], preferred_element_type=jnp.float32
        ).astype(jnp.bfloat16)

    def spread_hot_send(wave):
        def send(i, unused):
            to = to_member(i)
            hot_send[i] = spread_hot(to)
            remote(
                hot_send.at[i], hot_got.at[i], send_sem.at[4], recv_sem.at[4 + wave], (group, to)
            ).start()
            return unused

        return send

    half = MEMBERS // 2
    lax.fori_loop(1, half, spread_hot_send(0), 0)
    lax.fori_loop(half, MEMBERS, spread_hot_send(1), 0)
    hot_got[0] = spread_hot(member)

    def spread_cold(i):
        to = to_member(i)
        rows = jnp.concatenate(
            [slot_id[:CCAP] + (to_group[k] * MEMBERS + to) * CCAP for k in range(GROUPS)], axis=0
        )
        wanted = [cold_pos[table : table + 1, :] for table in range(TABLES)]
        sent = jnp.dot(one_hot(rows, wanted), terms[...], preferred_element_type=jnp.float32)
        cold_send[i] = sent.astype(jnp.bfloat16).reshape(GROUPS, CCAP, LANES)
        return to

    def send_cold(i, to, groups):
        wave = lax.div(i, MEMBERS // WAVES)
        for k in groups:
            remote(
                cold_send.at[i, k], cold_got.at[i * GROUPS + k], send_sem.at[5], cold_sem.at[wave],
                (to_group[k], to),
            ).start()

    def spread_cold_send(i, unused):
        send_cold(i, spread_cold(i), range(GROUPS))
        return unused

    send_cold(0, spread_cold(0), range(1, GROUPS))
    cold_got[0] = cold_send[0, 0]
    lax.fori_loop(1, half, spread_cold_send, 0)

    def add_hot(first, steps, total):
        for i in steps:
            asked = hot_asked[i] - first
            wanted = [asked[:, c * LANES : (c + 1) * LANES] for c in range(HCAP // LANES)]
            total = total + jnp.dot(
                one_hot(slot_id, wanted), hot_got[i], preferred_element_type=jnp.float32
            )
        return total

    drain(hot_got, 1, half - 1, send_sem.at[4], recv_sem.at[4]).wait_recv()

    def early(block, unused):
        partial[block] = add_hot(block * SLICE, range(half), jnp.zeros((SLICE, LANES), jnp.float32))
        return unused

    lax.fori_loop(0, GROUPS, early, 0)
    lax.fori_loop(half, MEMBERS, spread_cold_send, 0)
    drain(hot_got, half, MEMBERS - half, send_sem.at[4], recv_sem.at[5]).wait_recv()
    for k in list(range(1, GROUPS)) + [0]:
        to = to_group[k]
        total = add_hot(to * SLICE, range(half, MEMBERS), partial[to])
        if k == 0:
            own = total
        else:
            part_out[k] = total.astype(jnp.bfloat16)
            remote(
                part_out.at[k], part_got.at[k], send_sem.at[6], recv_sem.at[6], (to, member)
            ).start()
    partial[0] = own

    block_rows = 512
    per_wave = DEVICES // WAVES
    big_id = lax.broadcasted_iota(jnp.int32, (block_rows, LANES), 0)
    quarter = lax.div(lax.broadcasted_iota(jnp.int32, (1, LANES), 1), CCAP)

    def settle_cold(wave, first_wave):
        asked = []
        for c in range(per_wave // 4):
            row = cold_asked[wave * per_wave + 4 * c]
            for q in range(1, 4):
                row = jnp.where(quarter == q, cold_asked[wave * per_wave + 4 * c + q], row)
            asked.append(row)
        values = cold_got[pl.ds(wave * per_wave, per_wave)].reshape(per_wave * CCAP, LANES)

        def block(n, unused):
            first = pl.multiple_of(n * block_rows, block_rows)
            rows = pl.ds(first, block_rows)
            sums = jnp.dot(
                one_hot(big_id + first, asked), values, preferred_element_type=jnp.float32
            )
            cold_grad[rows, :] = sums if first_wave else cold_grad[rows, :] + sums
            return unused

        lax.fori_loop(0, COLD_ROWS // block_rows, block, 0)

    def cold_wave(wave, unused):
        drain(cold_got, wave * per_wave, per_wave, send_sem.at[5], cold_sem.at[wave]).wait_recv()
        settle_cold(wave, False)
        return unused

    drain(cold_got, 1, per_wave - 1, send_sem.at[5], cold_sem.at[0]).wait_recv()
    settle_cold(0, True)
    lax.fori_loop(1, 4, cold_wave, 0)

    drain(part_got, 1, GROUPS - 1, send_sem.at[6], recv_sem.at[6]).wait_recv()
    total = partial[0]
    for k in range(1, GROUPS):
        total = total + part_got[k].astype(jnp.float32)
    hot_grad[group] = total.astype(jnp.bfloat16)
    for k in range(1, GROUPS):
        remote(
            hot_grad.at[group], hot_grad.at[group], send_sem.at[7], recv_sem.at[7],
            (to_group[k], member),
        ).start()
    lax.fori_loop(4, WAVES, cold_wave, 0)

    drain(hot_asked, 1, MEMBERS - 1, send_sem.at[0], recv_sem.at[0]).wait_send()
    drain(cold_asked, 1, DEVICES - 1, send_sem.at[1], recv_sem.at[1]).wait_send()
    drain(hot_out, 1, MEMBERS - 1, send_sem.at[2], recv_sem.at[2]).wait_send()
    drain(cold_out, 1, DEVICES - 1, send_sem.at[3], recv_sem.at[3]).wait_send()
    drain(hot_send, 1, MEMBERS - 1, send_sem.at[4], recv_sem.at[4]).wait_send()
    drain(cold_got, 1, DEVICES - 1, send_sem.at[5], recv_sem.at[4]).wait_send()
    drain(part_out, 1, GROUPS - 1, send_sem.at[6], recv_sem.at[6]).wait_send()
    drain(hot_grad, 1, GROUPS - 1, send_sem.at[7], recv_sem.at[7]).wait()


def train(
    hot_request, cold_request, hot_pos, cold_pos, bottom, labels, w_out,
    hot_table, cold_table, w_first, w_second,
):
    i32 = jnp.int32
    hot_block, cold_block = (MEMBERS, HCAP, LANES), (DEVICES, CCAP, LANES)
    return pl.pallas_call(
        step_kernel,
        out_shape=[
            jax.ShapeDtypeStruct((GROUPS, SLICE, LANES), jnp.bfloat16),
            jax.ShapeDtypeStruct((COLD_ROWS, LANES), jnp.float32),
        ],
        in_specs=[VMEM] * 7 + [ANY] * 4,
        out_specs=[VMEM] * 2,
        scratch_shapes=[
            f32(HOT_ROWS, LANES), f32(COLD_ROWS, LANES), b16(*w_first.shape), b16(*w_second.shape),
            pltpu.VMEM((MEMBERS, 1, HCAP), i32), pltpu.VMEM((DEVICES, 1, LANES), i32),
            pltpu.SMEM((MEMBERS, 1, HCAP), i32), pltpu.SMEM((DEVICES, 1, LANES), i32),
            pltpu.SMEM((2 * TABLES, LANES), i32), pltpu.SMEM((TABLES, LANES), i32),
            b16(*hot_block), b16(*cold_block), b16(*hot_block), b16(*cold_block), f32(CCAP, LANES),
            f32(MEMBERS * HCAP, LANES), f32(DEVICES * CCAP, LANES),
            b16(LANES, w_first.shape[0]), f32(TABLES, LANES, LANES), b16(PAIRS, LANES),
            b16(*hot_block), b16(MEMBERS, GROUPS, CCAP, LANES), b16(*hot_block), b16(*cold_block),
            f32(GROUPS, SLICE, LANES), b16(GROUPS, SLICE, LANES), b16(GROUPS, SLICE, LANES),
            DMA((8,)), DMA((8,)), DMA((8,)), DMA((WAVES,)),
        ],
        compiler_params=pltpu.CompilerParams(
            collective_id=0, has_side_effects=True, vmem_limit_bytes=60 << 20
        ),
        name="step",
    )(
        hot_request, cold_request, hot_pos, cold_pos, bottom, labels, w_out,
        hot_table, cold_table, w_first, w_second,
    )


def update_kernel(gradient, acc, table, new_table, new_acc):
    first = lax.broadcasted_iota(jnp.int32, (LANES, LANES), 0)
    second = lax.broadcasted_iota(jnp.int32, (LANES, LANES), 1)
    diagonal = first == second
    for block in range(table.shape[0] // LANES):
        rows = slice(block * LANES, (block + 1) * LANES)
        grad = gradient[rows, :].astype(jnp.float32)
        spread_acc = jnp.where(diagonal, acc[block : block + 1, :], 0.0)
        new = jnp.sum(grad * grad * (1.0 / LANES) + spread_acc, axis=1, keepdims=True)
        new_table[rows, :] = table[rows, :] - STEP_RATE * grad * lax.rsqrt(new)
        new_acc[block : block + 1, :] = jnp.sum(jnp.where(diagonal, new, 0.0), axis=0, keepdims=True)


def update(gradient, acc, table, name):
    block = 1024
    rows = pl.BlockSpec((block, LANES), lambda n: (n, 0))
    packed = pl.BlockSpec((block // LANES, LANES), lambda n: (n, 0))
    return pl.pallas_call(
        update_kernel,
        grid=(table.shape[0] // block,),
        out_shape=[
            jax.ShapeDtypeStruct(table.shape, jnp.float32),
            jax.ShapeDtypeStruct(acc.shape, jnp.float32),
        ],
        in_specs=[rows, packed, rows],
        out_specs=[rows, packed],
        name=name,
    )(gradient, acc, table)


def shards(
    hot_table, hot_acc, cold_table, cold_acc, bottom_out, labels,
    hot_owner, hot_offset, cold_owner, cold_offset, w_first, w_second, w_out,
):
    def by_lane(lookups):
        return jnp.transpose(lookups, (1, 2, 0)).reshape(-1, LANES)

    hot_request, hot_pos, cold_request, cold_pos = place_all(
        by_lane(hot_owner), by_lane(hot_offset), by_lane(cold_owner), by_lane(cold_offset)
    )
    hot_grad, cold_grad = train(
        hot_request, cold_request, hot_pos, cold_pos, bottom_out, labels.reshape(1, -1),
        w_out.reshape(1, -1), hot_table, cold_table, w_first, w_second,
    )
    new_hot, new_hot_acc = update(
        hot_grad.reshape(-1, LANES), hot_acc.reshape(-1, LANES), hot_table, "update_hot"
    )
    new_cold, new_cold_acc = update(cold_grad, cold_acc.reshape(-1, LANES), cold_table, "update_cold")
    return (new_hot, new_hot_acc.reshape(-1), new_cold, new_cold_acc.reshape(-1))


def solution(mesh):
    both = P(("group", "member"))
    in_specs = (P("member"), P("member")) + (both,) * 8 + (P(),) * 3
    out_specs = (P("member"), P("member"), both, both)
    return jax.shard_map(shards, mesh=mesh, in_specs=in_specs, out_specs=out_specs, check_vma=False)
```

```python
import functools

import jax
import jax.numpy as jnp
from jax import lax
from jax.experimental import pallas as pl
from jax.experimental.pallas import tpu as pltpu
from jax.sharding import PartitionSpec as P

STEP_RATE = 0.5
LANES = 128
MEMBERS = 16
GROUPS = 8
DEVICES = 128
HOT_ROWS = 2048
COLD_ROWS = 4096
HCAP = 256
CCAP = 32
HIDDEN = 2048
TABLES = 8
SLICE = HOT_ROWS // GROUPS
MESH = pl.DeviceIdType.MESH
NT = (((1,), (1,)), ((), ()))

ANY = pl.BlockSpec(memory_space=pl.ANY)
DMA = pltpu.SemaphoreType.DMA


def f32(*shape):
    return pltpu.VMEM(shape, jnp.float32)


def b16(*shape):
    return pltpu.VMEM(shape, jnp.bfloat16)


def remote(src, dst, send, recv, to):
    return pltpu.make_async_remote_copy(
        src_ref=src, dst_ref=dst, send_sem=send, recv_sem=recv, device_id=to, device_id_type=MESH
    )


def place(owner_ref, offset_ref, owners, cap, table_rows, request_ref, position_ref):
    rows = owner_ref.shape[0]
    owner_ids = lax.broadcasted_iota(jnp.int32, (owners, LANES), 0)
    hits = [(owner_ref[r : r + 1, :] == owner_ids).astype(jnp.float32) for r in range(rows)]
    stacked = jnp.concatenate(hits, axis=0).astype(jnp.bfloat16)
    first = lax.broadcasted_iota(jnp.int32, (LANES, LANES), 0)
    second = lax.broadcasted_iota(jnp.int32, (LANES, LANES), 1)
    earlier = (first < second).astype(jnp.float32)
    side = jnp.concatenate([earlier, jnp.ones((LANES, LANES), jnp.float32)], axis=1)
    counts = jnp.dot(stacked, side.astype(jnp.bfloat16), preferred_element_type=jnp.float32)
    base = jnp.zeros((owners, LANES), jnp.float32)
    width = request_ref.shape[2]
    slots = lax.broadcasted_iota(jnp.int32, (width, LANES), 0) % cap
    high, low, at_slot = [], [], []
    for r in range(rows):
        count = counts[r * owners : (r + 1) * owners]
        slot = jnp.sum(hits[r] * (count[:, :LANES] + base), axis=0, keepdims=True).astype(jnp.int32)
        base = base + count[:, LANES:]
        position_ref[r : r + 1, :] = jnp.clip(
            owner_ref[r : r + 1, :] * cap + slot, 0, owners * cap - 1
        )
        offset = offset_ref[r : r + 1, :]
        high.append(hits[r] * (offset // 64).astype(jnp.float32))
        low.append(hits[r] * (offset % 64).astype(jnp.float32))
        at_slot.append((slots == slot).astype(jnp.float32).astype(jnp.bfloat16))
    digits = jnp.concatenate(
        [jnp.concatenate(high, axis=1), jnp.concatenate(low, axis=1)], axis=0
    ).astype(jnp.bfloat16)
    placed = lax.dot_general(
        digits, jnp.concatenate(at_slot, axis=1), NT, preferred_element_type=jnp.float32
    )
    requests = jnp.clip(
        (placed[:owners] * 64.0 + placed[owners:]).astype(jnp.int32), 0, table_rows - 1
    )
    for owner in range(owners):
        request_ref[owner] = requests[owner : owner + 1, :]


WAVES = 8
PAIRS = TABLES * LANES


def step_kernel(
    hot_owner_hbm, hot_offset_hbm, cold_owner_hbm, cold_offset_hbm, bottom_hbm, labels_hbm, out_hbm,
    hot_hbm, cold_hbm, first_hbm, second_hbm,
    hot_grad, cold_grad_hbm,
    hot_owner, hot_offset, cold_owner, cold_offset, labels, w_out,
    hot_request, cold_request, hot_pos, cold_pos, own_grad, cold_grad,
    hot_table, cold_table, w_first, w_second,
    hot_asked, cold_asked, hot_index, cold_index, hot_at, cold_at,
    hot_out, cold_out, hot_rows, cold_rows, stage, picked, hot_wide, cold_wide, features, pooled, terms,
    hot_send, cold_send, hot_got, cold_got, partial, part_out, part_got,
    local_sem, send_sem, recv_sem, cold_sem, present,
):
    group, member = lax.axis_index("group"), lax.axis_index("member")
    me = group * MEMBERS + member
    z, x, y, core = lax.div(member, 4), lax.rem(member, 4), lax.div(group, 2), lax.rem(group, 2)
    xs = [lax.rem(x + d, 4) for d in range(4)]
    zs = [lax.rem(z + d, 4) * 4 for d in range(4)]
    members = [zs[d // 4] + xs[d % 4] for d in range(MEMBERS)]
    ys = [lax.rem(y + d, 4) * 2 for d in range(4)]
    cores = [core, 1 - core]
    to_group = [ys[k // 2] + cores[k % 2] for k in range(GROUPS)]
    from_group = [ys[(4 - k // 2) % 4] + cores[k % 2] for k in range(GROUPS)]

    def member_step(i):
        step = lax.rem(i * 7, MEMBERS)
        return lax.div(step, 4), lax.rem(step, 4)

    def to_member(i):
        dz, dx = member_step(i)
        return lax.rem(z + dz, 4) * 4 + lax.rem(x + dx, 4)

    def from_member(i):
        dz, dx = member_step(i)
        return lax.rem(z + 4 - dz, 4) * 4 + lax.rem(x + 4 - dx, 4)

    def load(src, dst, n):
        copy = pltpu.make_async_copy(src, dst, local_sem.at[n])
        copy.start()
        return copy

    ids = [
        load(hot_owner_hbm, hot_owner, 0), load(hot_offset_hbm, hot_offset, 1),
        load(cold_owner_hbm, cold_owner, 2), load(cold_offset_hbm, cold_offset, 3),
    ]
    barrier = pltpu.get_barrier_semaphore()
    for d in range(1, MEMBERS):
        pl.semaphore_signal(barrier, inc=1, device_id=(group, members[d]), device_id_type=MESH)
    for k in range(1, GROUPS):
        pl.semaphore_signal(barrier, inc=1, device_id=(to_group[k], member), device_id_type=MESH)
    load_hot = load(hot_hbm, hot_table, 4)
    load_cold = load(cold_hbm, cold_table, 5)
    small = [
        load(bottom_hbm, features.at[:, pl.ds(0, LANES)], 6), load(labels_hbm, labels, 7),
        load(out_hbm, w_out, 8),
    ]
    load_first = load(first_hbm, w_first, 9)
    load_second = load(second_hbm, w_second, 10)
    ids[0].wait()
    ids[1].wait()
    place(hot_owner, hot_offset, MEMBERS, HCAP, HOT_ROWS, hot_request, hot_pos)
    pl.semaphore_wait(barrier, MEMBERS - 1 + GROUPS - 1)
    for k in range(1, GROUPS):
        pl.semaphore_signal(present, inc=1, device_id=(to_group[k], member), device_id_type=MESH)

    beside = (group, members[1])

    def drain(buffer, first, parts, send, recv):
        part = buffer.at[pl.ds(first, parts)]
        return remote(part, part, send, recv, beside)

    def ask_hot(i, unused):
        to = to_member(i)
        remote(
            hot_request.at[to], hot_asked.at[i], send_sem.at[0], recv_sem.at[0], (group, to)
        ).start()
        return unused

    lax.fori_loop(1, MEMBERS, ask_hot, 0)

    hot_asked[0] = hot_request[member]
    ids[2].wait()
    ids[3].wait()
    place(cold_owner, cold_offset, DEVICES, CCAP, COLD_ROWS, cold_request, cold_pos)
    index_loads = [load(hot_pos, hot_at, 11), load(cold_pos, cold_at, 12)]
    pl.semaphore_wait(present, GROUPS - 1)

    def ask_cold_at(i, groups):
        to = to_member(i)
        for k in groups:
            remote(
                cold_request.at[to_group[k] * MEMBERS + to], cold_asked.at[i * GROUPS + k],
                send_sem.at[1], recv_sem.at[1], (to_group[k], to),
            ).start()

    def ask_cold(i, unused):
        ask_cold_at(i, range(GROUPS))
        return unused

    ask_cold_at(0, range(1, GROUPS))
    lax.fori_loop(1, MEMBERS, ask_cold, 0)
    cold_asked[0] = cold_request[me]

    drain(hot_asked, 1, MEMBERS - 1, send_sem.at[0], recv_sem.at[0]).wait_recv()
    to_scalars = load(hot_asked, hot_index, 13)
    load_hot.wait()
    to_scalars.wait()

    def pick(table, index, row, first, target):
        for j in range(CCAP):
            stage[pl.ds(j, 1), :] = table[pl.ds(index[row, 0, first + j], 1), :]
        target[...] = stage[...].astype(jnp.bfloat16)

    def serve_hot(i, target):
        def chunk(c, unused):
            first = pl.multiple_of(c * CCAP, CCAP)
            pick(hot_table, hot_index, i, first, target.at[pl.ds(first, CCAP), :])
            return unused

        lax.fori_loop(0, HCAP // CCAP, chunk, 0)

    def serve_hot_send(i, unused):
        to = from_member(i)
        serve_hot(i, hot_out.at[i])
        remote(
            hot_out.at[i], hot_rows.at[member], send_sem.at[2], recv_sem.at[2], (group, to)
        ).start()
        return unused

    lax.fori_loop(1, MEMBERS, serve_hot_send, 0)
    serve_hot(0, hot_rows.at[member])

    drain(cold_asked, 1, DEVICES - 1, send_sem.at[1], recv_sem.at[1]).wait_recv()
    to_scalars = load(cold_asked, cold_index, 14)
    load_cold.wait()
    to_scalars.wait()

    def serve_cold_at(i, groups):
        to = from_member(i)
        for k in groups:
            n = i * GROUPS + k
            pick(cold_table, cold_index, n, 0, cold_out.at[n])
            remote(
                cold_out.at[n], cold_rows.at[me], send_sem.at[3], recv_sem.at[3],
                (from_group[k], to),
            ).start()

    def serve_cold(i, unused):
        serve_cold_at(i, range(GROUPS))
        return unused

    serve_cold_at(0, range(1, GROUPS))
    lax.fori_loop(1, MEMBERS, serve_cold, 0)
    pick(cold_table, cold_index, 0, 0, cold_rows.at[me])

    for copy in index_loads + small:
        copy.wait()
    unroll = 16
    drain(hot_rows, 0, MEMBERS - 1, send_sem.at[2], recv_sem.at[2]).wait_recv()
    hot_wide[...] = hot_rows[...].astype(jnp.float32).reshape(hot_wide.shape)
    for table in range(TABLES):

        def combine_hot(k, unused):
            for j in range(unroll):
                b = k * unroll + j
                pooled[table, pl.ds(b, 1), :] = (
                    hot_wide[pl.ds(hot_at[2 * table, b], 1), :]
                    + hot_wide[pl.ds(hot_at[2 * table + 1, b], 1), :]
                )
            return unused

        lax.fori_loop(0, LANES // unroll, combine_hot, 0)
    drain(cold_rows, 0, DEVICES - 1, send_sem.at[3], recv_sem.at[3]).wait_recv()
    cold_wide[...] = cold_rows[...].astype(jnp.float32).reshape(cold_wide.shape)
    for table in range(TABLES):

        def combine_cold(k, unused):
            for j in range(unroll):
                b = k * unroll + j
                picked[pl.ds(b, 1), :] = cold_wide[pl.ds(cold_at[table, b], 1), :]
            return unused

        lax.fori_loop(0, LANES // unroll, combine_cold, 0)
        features[:, (table + 1) * LANES : (table + 2) * LANES] = (
            pooled[table] + picked[...]
        ).astype(jnp.bfloat16)

    load_first.wait()
    first_pre = jnp.dot(features[...], w_first[...], preferred_element_type=jnp.float32)
    first_act = jnp.maximum(first_pre, 0.0).astype(jnp.bfloat16)
    load_second.wait()
    second_pre = jnp.dot(first_act, w_second[...], preferred_element_type=jnp.float32)
    second_act = jnp.maximum(second_pre, 0.0).astype(jnp.bfloat16)
    out_wide = w_out[...].astype(jnp.float32).reshape(1, -1)
    score = jnp.sum(second_act.astype(jnp.float32) * out_wide, axis=1, keepdims=True)
    row_id = lax.broadcasted_iota(jnp.int32, (LANES, LANES), 0)
    lane_id = lax.broadcasted_iota(jnp.int32, (LANES, LANES), 1)
    label = jnp.sum(jnp.where(row_id == lane_id, labels[...], 0.0), axis=1, keepdims=True)
    delta = jax.nn.sigmoid(score) - label
    grad_second = jnp.where(second_pre > 0, delta * out_wide, 0.0).astype(jnp.bfloat16)
    back_second = lax.dot_general(grad_second, w_second[...], NT, preferred_element_type=jnp.float32)
    grad_first = jnp.where(first_pre > 0, back_second, 0.0).astype(jnp.bfloat16)
    for table in range(TABLES):
        terms[table * LANES : (table + 1) * LANES, :] = lax.dot_general(
            grad_first, w_first[(table + 1) * LANES : (table + 2) * LANES, :], NT,
            preferred_element_type=jnp.float32,
        ).astype(jnp.bfloat16)

    slot_id = lax.broadcasted_iota(jnp.int32, (HCAP, LANES), 0)

    def one_hot(rows, wanted):
        return jnp.concatenate([jnp.where(rows == w, 1.0, 0.0).astype(jnp.bfloat16) for w in wanted], axis=1)

    def spread_hot(to):
        base = to * HCAP
        wanted = []
        for table in range(TABLES):
            one = hot_pos[2 * table : 2 * table + 1, :] - base
            two = hot_pos[2 * table + 1 : 2 * table + 2, :] - base
            wanted.append(jnp.where((one >= 0) & (one < HCAP), one, two))
        return jnp.dot(
            one_hot(slot_id, wanted), terms[...], preferred_element_type=jnp.float32
        ).astype(jnp.bfloat16)

    def spread_hot_send(wave):
        def send(i, unused):
            to = to_member(i)
            hot_send[i] = spread_hot(to)
            remote(
                hot_send.at[i], hot_got.at[i], send_sem.at[4], recv_sem.at[4 + wave], (group, to)
            ).start()
            return unused

        return send

    half = MEMBERS // 2
    lax.fori_loop(1, half, spread_hot_send(0), 0)
    lax.fori_loop(half, MEMBERS, spread_hot_send(1), 0)
    hot_got[0] = spread_hot(member)

    def spread_cold(i):
        to = to_member(i)
        rows = jnp.concatenate(
            [slot_id[:CCAP] + (to_group[k] * MEMBERS + to) * CCAP for k in range(GROUPS)], axis=0
        )
        wanted = [cold_pos[table : table + 1, :] for table in range(TABLES)]
        sent = jnp.dot(one_hot(rows, wanted), terms[...], preferred_element_type=jnp.float32)
        cold_send[i] = sent.astype(jnp.bfloat16).reshape(GROUPS, CCAP, LANES)

    def send_cold(i, to, groups):
        wave = lax.div(i, MEMBERS // WAVES)
        for k in groups:
            remote(
                cold_send.at[i, k], cold_got.at[i * GROUPS + k], send_sem.at[5], cold_sem.at[wave],
                (to_group[k], to),
            ).start()

    def spread_only(i, unused):
        spread_cold(i)
        return unused

    def send_only(i, unused):
        send_cold(i, to_member(i), range(GROUPS))
        return unused

    lax.fori_loop(0, MEMBERS, spread_only, 0)
    cold_got[0] = cold_send[0, 0]

    def add_hot(first, steps, total):
        for i in steps:
            asked = hot_asked[i] - first
            wanted = [asked[:, c * LANES : (c + 1) * LANES] for c in range(HCAP // LANES)]
            total = total + jnp.dot(
                one_hot(slot_id, wanted), hot_got[i], preferred_element_type=jnp.float32
            )
        return total

    drain(hot_got, 1, half - 1, send_sem.at[4], recv_sem.at[4]).wait_recv()
    send_cold(0, member, range(1, GROUPS))
    lax.fori_loop(1, half, send_only, 0)

    def early(block, unused):
        partial[block] = add_hot(block * SLICE, range(half), jnp.zeros((SLICE, LANES), jnp.float32))
        return unused

    lax.fori_loop(0, GROUPS, early, 0)
    lax.fori_loop(half, MEMBERS, send_only, 0)
    drain(hot_got, half, MEMBERS - half, send_sem.at[4], recv_sem.at[5]).wait_recv()
    for k in list(range(1, GROUPS)) + [0]:
        to = to_group[k]
        total = add_hot(to * SLICE, range(half, MEMBERS), partial[to])
        if k == 0:
            own = total
        else:
            part_out[k] = total.astype(jnp.bfloat16)
            remote(
                part_out.at[k], part_got.at[k], send_sem.at[6], recv_sem.at[6], (to, member)
            ).start()
    partial[0] = own

    block_rows = 512
    per_wave = DEVICES // WAVES
    big_id = lax.broadcasted_iota(jnp.int32, (block_rows, LANES), 0)
    quarter = lax.div(lax.broadcasted_iota(jnp.int32, (1, LANES), 1), CCAP)

    def settle_cold(wave, first_wave):
        asked = []
        for c in range(per_wave // 4):
            row = cold_asked[wave * per_wave + 4 * c]
            for q in range(1, 4):
                row = jnp.where(quarter == q, cold_asked[wave * per_wave + 4 * c + q], row)
            asked.append(row)
        values = cold_got[pl.ds(wave * per_wave, per_wave)].reshape(per_wave * CCAP, LANES)

        def block(n, unused):
            first = pl.multiple_of(n * block_rows, block_rows)
            rows = pl.ds(first, block_rows)
            sums = jnp.dot(
                one_hot(big_id + first, asked), values, preferred_element_type=jnp.float32
            )
            cold_grad[rows, :] = sums if first_wave else cold_grad[rows, :] + sums
            return unused

        lax.fori_loop(0, COLD_ROWS // block_rows, block, 0)

    def cold_wave(wave, unused):
        drain(cold_got, wave * per_wave, per_wave, send_sem.at[5], cold_sem.at[wave]).wait_recv()
        settle_cold(wave, False)
        return unused

    drain(cold_got, 1, per_wave - 1, send_sem.at[5], cold_sem.at[0]).wait_recv()
    settle_cold(0, True)
    lax.fori_loop(1, 3, cold_wave, 0)

    drain(part_got, 1, GROUPS - 1, send_sem.at[6], recv_sem.at[6]).wait_recv()
    total = partial[0]
    for k in range(1, GROUPS):
        total = total + part_got[k].astype(jnp.float32)
    own_grad[...] = total.astype(jnp.bfloat16)
    keep_own = load(own_grad, hot_grad.at[group], 15)
    for k in range(1, GROUPS):
        remote(
            own_grad, hot_grad.at[group], send_sem.at[7], recv_sem.at[7],
            (to_group[k], member),
        ).start()
    lax.fori_loop(3, WAVES, cold_wave, 0)
    keep_cold = load(cold_grad, cold_grad_hbm, 16)
    keep_own.wait()
    keep_cold.wait()

    drain(hot_asked, 1, MEMBERS - 1, send_sem.at[0], recv_sem.at[0]).wait_send()
    drain(cold_asked, 1, DEVICES - 1, send_sem.at[1], recv_sem.at[1]).wait_send()
    drain(hot_out, 1, MEMBERS - 1, send_sem.at[2], recv_sem.at[2]).wait_send()
    drain(cold_out, 1, DEVICES - 1, send_sem.at[3], recv_sem.at[3]).wait_send()
    drain(hot_send, 1, MEMBERS - 1, send_sem.at[4], recv_sem.at[4]).wait_send()
    drain(cold_got, 1, DEVICES - 1, send_sem.at[5], recv_sem.at[4]).wait_send()
    drain(part_out, 1, GROUPS - 1, send_sem.at[6], recv_sem.at[6]).wait_send()
    drain(hot_grad, 1, GROUPS - 1, send_sem.at[7], recv_sem.at[7]).wait()


def train(
    hot_owner, hot_offset, cold_owner, cold_offset, bottom, labels, w_out,
    hot_table, cold_table, w_first, w_second,
):
    i32 = jnp.int32
    hot_block, cold_block = (MEMBERS, HCAP, LANES), (DEVICES, CCAP, LANES)
    return pl.pallas_call(
        step_kernel,
        out_shape=[
            jax.ShapeDtypeStruct((GROUPS, SLICE, LANES), jnp.bfloat16),
            jax.ShapeDtypeStruct((COLD_ROWS, LANES), jnp.float32),
        ],
        in_specs=[ANY] * 11,
        out_specs=[ANY] * 2,
        scratch_shapes=[
            pltpu.VMEM((2 * TABLES, LANES), i32), pltpu.VMEM((2 * TABLES, LANES), i32),
            pltpu.VMEM((TABLES, LANES), i32), pltpu.VMEM((TABLES, LANES), i32),
            f32(1, LANES), b16(*w_out.shape),
            pltpu.VMEM((MEMBERS, 1, HCAP), i32), pltpu.VMEM((DEVICES, 1, LANES), i32),
            pltpu.VMEM((2 * TABLES, LANES), i32), pltpu.VMEM((TABLES, LANES), i32),
            b16(SLICE, LANES), f32(COLD_ROWS, LANES),
            f32(HOT_ROWS, LANES), f32(COLD_ROWS, LANES), b16(*w_first.shape), b16(*w_second.shape),
            pltpu.VMEM((MEMBERS, 1, HCAP), i32), pltpu.VMEM((DEVICES, 1, LANES), i32),
            pltpu.SMEM((MEMBERS, 1, HCAP), i32), pltpu.SMEM((DEVICES, 1, LANES), i32),
            pltpu.SMEM((2 * TABLES, LANES), i32), pltpu.SMEM((TABLES, LANES), i32),
            b16(*hot_block), b16(*cold_block), b16(*hot_block), b16(*cold_block), f32(CCAP, LANES),
            f32(LANES, LANES), f32(MEMBERS * HCAP, LANES), f32(DEVICES * CCAP, LANES),
            b16(LANES, w_first.shape[0]), f32(TABLES, LANES, LANES), b16(PAIRS, LANES),
            b16(*hot_block), b16(MEMBERS, GROUPS, CCAP, LANES), b16(*hot_block), b16(*cold_block),
            f32(GROUPS, SLICE, LANES), b16(GROUPS, SLICE, LANES), b16(GROUPS, SLICE, LANES),
            DMA((17,)), DMA((8,)), DMA((8,)), DMA((WAVES,)), pltpu.SemaphoreType.REGULAR,
        ],
        compiler_params=pltpu.CompilerParams(
            collective_id=0, has_side_effects=True, vmem_limit_bytes=62 << 20
        ),
        name="step",
    )(
        hot_owner, hot_offset, cold_owner, cold_offset, bottom, labels, w_out,
        hot_table, cold_table, w_first, w_second,
    )


def split(value, parts):
    found = []
    for _ in range(parts):
        part = value.astype(jnp.bfloat16)
        found.append(part)
        value = value - part.astype(jnp.float32)
    return found


def update_kernel(
    hot_grad, hot_acc, hot_table, cold_grad, cold_acc, cold_table,
    new_hot, new_hot_acc, new_cold, new_cold_acc,
):
    first = lax.broadcasted_iota(jnp.int32, (LANES, LANES), 0)
    second = lax.broadcasted_iota(jnp.int32, (LANES, LANES), 1)
    diagonal = first == second
    weights = jnp.concatenate(
        [jnp.full((2 * LANES, LANES), 1.0 / LANES), jnp.ones((3 * LANES, LANES))], axis=0
    ).astype(jnp.bfloat16)

    def adagrad(gradient, acc, table, new_table, new_acc):
        for block in range(table.shape[0] // LANES):
            rows = slice(block * LANES, (block + 1) * LANES)
            grad = gradient[rows, :].astype(jnp.float32)
            spread_acc = jnp.where(diagonal, acc[0, block : block + 1, :], 0.0)
            parts = jnp.concatenate(split(grad * grad, 2) + split(spread_acc, 3), axis=1)
            new = jnp.dot(parts, weights, preferred_element_type=jnp.float32)
            new_table[rows, :] = table[rows, :] - STEP_RATE * grad * lax.rsqrt(new)
            new_acc[0, block : block + 1, :] = jnp.sum(
                jnp.where(diagonal, new, 0.0), axis=0, keepdims=True
            )

    adagrad(hot_grad, hot_acc, hot_table, new_hot, new_hot_acc)
    adagrad(cold_grad, cold_acc, cold_table, new_cold, new_cold_acc)


def update(hot_grad, hot_acc, hot_table, cold_grad, cold_acc, cold_table):
    steps = 4
    in_specs, out_specs, out_shape = [], [], []
    for table in (hot_table, cold_table):
        block = table.shape[0] // steps
        rows = pl.BlockSpec((block, LANES), lambda n: (n, 0))
        packed = pl.BlockSpec((1, block // LANES, LANES), lambda n: (n, 0, 0))
        in_specs += [rows, packed, rows]
        out_specs += [rows, packed]
        out_shape += [
            jax.ShapeDtypeStruct(table.shape, jnp.float32),
            jax.ShapeDtypeStruct((steps, block // LANES, LANES), jnp.float32),
        ]
    return pl.pallas_call(
        update_kernel,
        grid=(steps,),
        out_shape=out_shape,
        in_specs=in_specs,
        out_specs=out_specs,
        compiler_params=pltpu.CompilerParams(vmem_limit_bytes=62 << 20),
        name="update",
    )(
        hot_grad, hot_acc.reshape(steps, -1, LANES), hot_table,
        cold_grad, cold_acc.reshape(steps, -1, LANES), cold_table,
    )


def shards(
    hot_table, hot_acc, cold_table, cold_acc, bottom_out, labels,
    hot_owner, hot_offset, cold_owner, cold_offset, w_first, w_second, w_out,
):
    def by_lane(lookups):
        return jnp.transpose(lookups, (1, 2, 0)).reshape(-1, LANES)

    hot_grad, cold_grad = train(
        by_lane(hot_owner), by_lane(hot_offset), by_lane(cold_owner), by_lane(cold_offset),
        bottom_out, labels.reshape(1, -1), w_out, hot_table, cold_table, w_first, w_second,
    )
    new_hot, new_hot_acc, new_cold, new_cold_acc = update(
        hot_grad.reshape(-1, LANES), hot_acc, hot_table, cold_grad, cold_acc, cold_table
    )
    return (new_hot, new_hot_acc.reshape(-1), new_cold, new_cold_acc.reshape(-1))


def solution(mesh):
    both = P(("group", "member"))
    in_specs = (P("member"), P("member")) + (both,) * 8 + (P(),) * 3
    out_specs = (P("member"), P("member"), both, both)
    return jax.shard_map(shards, mesh=mesh, in_specs=in_specs, out_specs=out_specs, check_vma=False)
```

```python
import functools

import jax
import jax.numpy as jnp
from jax import lax
from jax.experimental import pallas as pl
from jax.experimental.pallas import tpu as pltpu
from jax.sharding import PartitionSpec as P

STEP_RATE = 0.5
LANES = 128
MEMBERS = 16
GROUPS = 8
DEVICES = 128
HOT_ROWS = 2048
COLD_ROWS = 4096
HCAP = 256
CCAP = 32
HIDDEN = 2048
TABLES = 8
SLICE = HOT_ROWS // GROUPS
MESH = pl.DeviceIdType.MESH
NT = (((1,), (1,)), ((), ()))

ANY = pl.BlockSpec(memory_space=pl.ANY)
DMA = pltpu.SemaphoreType.DMA


def f32(*shape):
    return pltpu.VMEM(shape, jnp.float32)


def b16(*shape):
    return pltpu.VMEM(shape, jnp.bfloat16)


def remote(src, dst, send, recv, to):
    return pltpu.make_async_remote_copy(
        src_ref=src, dst_ref=dst, send_sem=send, recv_sem=recv, device_id=to, device_id_type=MESH
    )


def place(owner_ref, offset_ref, owners, cap, table_rows, request_ref, position_ref):
    rows = owner_ref.shape[0]
    owner_ids = lax.broadcasted_iota(jnp.int32, (owners, LANES), 0)
    hits = [(owner_ref[r : r + 1, :] == owner_ids).astype(jnp.float32) for r in range(rows)]
    stacked = jnp.concatenate(hits, axis=0).astype(jnp.bfloat16)
    first = lax.broadcasted_iota(jnp.int32, (LANES, LANES), 0)
    second = lax.broadcasted_iota(jnp.int32, (LANES, LANES), 1)
    earlier = (first < second).astype(jnp.float32)
    side = jnp.concatenate([earlier, jnp.ones((LANES, LANES), jnp.float32)], axis=1)
    counts = jnp.dot(stacked, side.astype(jnp.bfloat16), preferred_element_type=jnp.float32)
    base = jnp.zeros((owners, LANES), jnp.float32)
    width = request_ref.shape[2]
    slots = lax.broadcasted_iota(jnp.int32, (width, LANES), 0) % cap
    high, low, at_slot = [], [], []
    for r in range(rows):
        count = counts[r * owners : (r + 1) * owners]
        slot = jnp.sum(hits[r] * (count[:, :LANES] + base), axis=0, keepdims=True).astype(jnp.int32)
        base = base + count[:, LANES:]
        position_ref[r : r + 1, :] = jnp.clip(
            owner_ref[r : r + 1, :] * cap + slot, 0, owners * cap - 1
        )
        offset = offset_ref[r : r + 1, :]
        high.append(hits[r] * (offset // 64).astype(jnp.float32))
        low.append(hits[r] * (offset % 64).astype(jnp.float32))
        at_slot.append((slots == slot).astype(jnp.float32).astype(jnp.bfloat16))
    digits = jnp.concatenate(
        [jnp.concatenate(high, axis=1), jnp.concatenate(low, axis=1)], axis=0
    ).astype(jnp.bfloat16)
    placed = lax.dot_general(
        digits, jnp.concatenate(at_slot, axis=1), NT, preferred_element_type=jnp.float32
    )
    requests = jnp.clip(
        (placed[:owners] * 64.0 + placed[owners:]).astype(jnp.int32), 0, table_rows - 1
    )
    for owner in range(owners):
        request_ref[owner] = requests[owner : owner + 1, :]


WAVES = 8
CLASSES = 4
HOT_CLASS = HOT_ROWS // CLASSES
COLD_CLASS = COLD_ROWS // CLASSES
PAIRS = TABLES * LANES


def step_kernel(
    hot_owner_hbm, hot_offset_hbm, cold_owner_hbm, cold_offset_hbm, bottom_hbm, labels_hbm, out_hbm,
    hot_hbm, cold_hbm, first_hbm, second_hbm,
    hot_grad, cold_grad_hbm,
    hot_owner, hot_offset, cold_owner, cold_offset, labels, w_out,
    hot_request, cold_request, hot_pos, cold_pos, own_grad, cold_grad,
    hot_table, cold_table, w_first, w_second,
    hot_asked, cold_asked, cold_asked_mid, hot_index, cold_index, hot_at, cold_at,
    hot_out, cold_out, hot_rows, cold_rows, stage, picked, hot_wide, cold_wide, features, pooled, terms,
    hot_send, cold_send, cold_mid, hot_got, cold_got, partial, part_out, part_got,
    hot_ids, cold_ids, hot_mask, cold_mask, wide_values,
    local_sem, send_sem, recv_sem, cold_sem, present,
):
    group, member = lax.axis_index("group"), lax.axis_index("member")
    me = group * MEMBERS + member
    z, x, y, core = lax.div(member, 4), lax.rem(member, 4), lax.div(group, 2), lax.rem(group, 2)
    xs = [lax.rem(x + d, 4) for d in range(4)]
    zs = [lax.rem(z + d, 4) * 4 for d in range(4)]
    members = [zs[d // 4] + xs[d % 4] for d in range(MEMBERS)]
    ys = [lax.rem(y + d, 4) * 2 for d in range(4)]
    cores = [core, 1 - core]
    to_group = [ys[k // 2] + cores[k % 2] for k in range(GROUPS)]
    from_group = [ys[(4 - k // 2) % 4] + cores[k % 2] for k in range(GROUPS)]

    def member_step(i):
        step = lax.rem(i * 7, MEMBERS)
        return lax.div(step, 4), lax.rem(step, 4)

    def to_member(i):
        dz, dx = member_step(i)
        return lax.rem(z + dz, 4) * 4 + lax.rem(x + dx, 4)

    def from_member(i):
        dz, dx = member_step(i)
        return lax.rem(z + 4 - dz, 4) * 4 + lax.rem(x + 4 - dx, 4)

    def load(src, dst, n):
        copy = pltpu.make_async_copy(src, dst, local_sem.at[n])
        copy.start()
        return copy

    ids = [
        load(hot_owner_hbm, hot_owner, 0), load(hot_offset_hbm, hot_offset, 1),
        load(cold_owner_hbm, cold_owner, 2), load(cold_offset_hbm, cold_offset, 3),
    ]
    barrier = pltpu.get_barrier_semaphore()
    for d in range(1, MEMBERS):
        pl.semaphore_signal(barrier, inc=1, device_id=(group, members[d]), device_id_type=MESH)
    for k in range(1, GROUPS):
        pl.semaphore_signal(barrier, inc=1, device_id=(to_group[k], member), device_id_type=MESH)
    load_hot = load(hot_hbm, hot_table, 4)
    load_cold = load(cold_hbm, cold_table, 5)
    small = [
        load(bottom_hbm, features.at[:, pl.ds(0, LANES)], 6), load(labels_hbm, labels, 7),
        load(out_hbm, w_out, 8),
    ]
    load_first = load(first_hbm, w_first, 9)
    load_second = load(second_hbm, w_second, 10)
    ids[0].wait()
    ids[1].wait()
    place(hot_owner, hot_offset, MEMBERS, HCAP, HOT_ROWS, hot_request, hot_pos)
    pl.semaphore_wait(barrier, MEMBERS - 1 + GROUPS - 1)
    for k in range(1, GROUPS):
        pl.semaphore_signal(present, inc=1, device_id=(to_group[k], member), device_id_type=MESH)

    beside = (group, members[1])

    def drain(buffer, first, parts, send, recv):
        part = buffer.at[pl.ds(first, parts)]
        return remote(part, part, send, recv, beside)

    def ask_hot(i, unused):
        to = to_member(i)
        remote(
            hot_request.at[to], hot_asked.at[i], send_sem.at[0], recv_sem.at[0], (group, to)
        ).start()
        return unused

    lax.fori_loop(1, MEMBERS, ask_hot, 0)
    hot_asked[0] = hot_request[member]
    ids[2].wait()
    ids[3].wait()
    place(cold_owner, cold_offset, DEVICES, CCAP, COLD_ROWS, cold_request, cold_pos)
    index_loads = [load(hot_pos, hot_at, 11), load(cold_pos, cold_at, 12)]
    for k in range(1, GROUPS):
        remote(
            cold_request.at[pl.ds(to_group[k] * MEMBERS, MEMBERS)], cold_asked_mid.at[:, k],
            send_sem.at[1], recv_sem.at[1], (to_group[k], member),
        ).start()
    cold_asked_mid[:, 0] = cold_request[pl.ds(group * MEMBERS, MEMBERS)]

    drain(hot_asked, 1, MEMBERS - 1, send_sem.at[0], recv_sem.at[0]).wait_recv()
    to_scalars = load(hot_asked, hot_index, 13)
    load_hot.wait()
    to_scalars.wait()

    def pick(table, index, row, first, target):
        for j in range(CCAP):
            stage[pl.ds(j, 1), :] = table[pl.ds(index[row, 0, first + j], 1), :]
        target[...] = stage[...].astype(jnp.bfloat16)

    def serve_hot(i, target):
        def chunk(c, unused):
            first = pl.multiple_of(c * CCAP, CCAP)
            pick(hot_table, hot_index, i, first, target.at[pl.ds(first, CCAP), :])
            return unused

        lax.fori_loop(0, HCAP // CCAP, chunk, 0)

    def serve_hot_send(i, unused):
        to = from_member(i)
        serve_hot(i, hot_out.at[i])
        remote(
            hot_out.at[i], hot_rows.at[member], send_sem.at[2], recv_sem.at[2], (group, to)
        ).start()
        return unused

    def ask_cold(i, unused):
        to = to_member(i)
        remote(
            cold_asked_mid.at[to], cold_asked.at[pl.ds(i * GROUPS, GROUPS)],
            send_sem.at[8], recv_sem.at[8], (group, to),
        ).start()
        return unused

    lax.fori_loop(1, 5, serve_hot_send, 0)
    drain(cold_asked, 0, DEVICES - MEMBERS, send_sem.at[1], recv_sem.at[1]).wait_recv()
    lax.fori_loop(1, MEMBERS, ask_cold, 0)
    cold_asked[pl.ds(0, GROUPS)] = cold_asked_mid[member]
    lax.fori_loop(5, MEMBERS, serve_hot_send, 0)
    serve_hot(0, hot_rows.at[member])

    drain(cold_asked, 0, DEVICES - GROUPS, send_sem.at[8], recv_sem.at[8]).wait_recv()
    to_scalars = load(cold_asked, cold_index, 14)
    load_cold.wait()
    to_scalars.wait()
    pl.semaphore_wait(present, GROUPS - 1)

    def serve_cold_at(i, groups):
        to = from_member(i)
        for k in groups:
            n = i * GROUPS + k
            pick(cold_table, cold_index, n, 0, cold_out.at[n])
            remote(
                cold_out.at[n], cold_rows.at[me], send_sem.at[3], recv_sem.at[3],
                (from_group[k], to),
            ).start()

    def serve_cold(i, unused):
        serve_cold_at(i, range(GROUPS))
        return unused

    serve_cold_at(0, range(1, GROUPS))
    lax.fori_loop(1, MEMBERS, serve_cold, 0)
    pick(cold_table, cold_index, 0, 0, cold_rows.at[me])

    for copy in index_loads + small:
        copy.wait()
    unroll = 16
    drain(hot_rows, 0, MEMBERS - 1, send_sem.at[2], recv_sem.at[2]).wait_recv()
    hot_wide[...] = hot_rows[...].astype(jnp.float32).reshape(hot_wide.shape)
    for table in range(TABLES):

        def combine_hot(k, unused):
            for j in range(unroll):
                b = k * unroll + j
                pooled[table, pl.ds(b, 1), :] = (
                    hot_wide[pl.ds(hot_at[2 * table, b], 1), :]
                    + hot_wide[pl.ds(hot_at[2 * table + 1, b], 1), :]
                )
            return unused

        lax.fori_loop(0, LANES // unroll, combine_hot, 0)
    row_id = lax.broadcasted_iota(jnp.int32, (LANES, LANES), 0)
    lane_id = lax.broadcasted_iota(jnp.int32, (LANES, LANES), 1)
    diagonal = row_id == lane_id
    ones = jnp.ones((LANES, LANES), jnp.bfloat16)
    quarter = lax.div(lax.broadcasted_iota(jnp.int32, (1, LANES), 1), CCAP)

    def note(asked, size, n, ids, mask):
        ids[n] = lax.rem(asked, size)
        which = lax.div(asked, size).astype(jnp.float32)
        wide = jnp.dot(
            jnp.where(diagonal, which, 0.0).astype(jnp.bfloat16), ones,
            preferred_element_type=jnp.float32,
        )
        for q in range(CLASSES):
            mask[q, n] = jnp.where(wide == q, 1.0, 0.0).astype(jnp.bfloat16)

    def note_hot(i, unused):
        for c in range(HCAP // LANES):
            asked = hot_asked[i][:, c * LANES : (c + 1) * LANES]
            note(asked, HOT_CLASS, i * (HCAP // LANES) + c, hot_ids, hot_mask)
        return unused

    def note_cold(n, unused):
        asked = cold_asked[4 * n]
        for q in range(1, 4):
            asked = jnp.where(quarter == q, cold_asked[4 * n + q], asked)
        note(asked, COLD_CLASS, n, cold_ids, cold_mask)
        return unused

    lax.fori_loop(0, MEMBERS, note_hot, 0)
    lax.fori_loop(0, DEVICES // 4, note_cold, 0)
    drain(cold_rows, 0, DEVICES - 1, send_sem.at[3], recv_sem.at[3]).wait_recv()
    cold_wide[...] = cold_rows[...].astype(jnp.float32).reshape(cold_wide.shape)
    for table in range(TABLES):

        def combine_cold(k, unused):
            for j in range(unroll):
                b = k * unroll + j
                picked[pl.ds(b, 1), :] = cold_wide[pl.ds(cold_at[table, b], 1), :]
            return unused

        lax.fori_loop(0, LANES // unroll, combine_cold, 0)
        features[:, (table + 1) * LANES : (table + 2) * LANES] = (
            pooled[table] + picked[...]
        ).astype(jnp.bfloat16)

    load_first.wait()
    first_pre = jnp.dot(features[...], w_first[...], preferred_element_type=jnp.float32)
    first_act = jnp.maximum(first_pre, 0.0).astype(jnp.bfloat16)
    load_second.wait()
    second_pre = jnp.dot(first_act, w_second[...], preferred_element_type=jnp.float32)
    second_act = jnp.maximum(second_pre, 0.0).astype(jnp.bfloat16)
    out_wide = w_out[...].astype(jnp.float32).reshape(1, -1)
    score = jnp.sum(second_act.astype(jnp.float32) * out_wide, axis=1, keepdims=True)
    label = jnp.sum(jnp.where(diagonal, labels[...], 0.0), axis=1, keepdims=True)
    delta = jax.nn.sigmoid(score) - label
    grad_second = jnp.where(second_pre > 0, delta * out_wide, 0.0).astype(jnp.bfloat16)
    back_second = lax.dot_general(grad_second, w_second[...], NT, preferred_element_type=jnp.float32)
    grad_first = jnp.where(first_pre > 0, back_second, 0.0).astype(jnp.bfloat16)
    for table in range(TABLES):
        terms[table * LANES : (table + 1) * LANES, :] = lax.dot_general(
            grad_first, w_first[(table + 1) * LANES : (table + 2) * LANES, :], NT,
            preferred_element_type=jnp.float32,
        ).astype(jnp.bfloat16)

    slot_id = lax.broadcasted_iota(jnp.int32, (HCAP, LANES), 0)

    def one_hot(rows, wanted):
        return jnp.concatenate([jnp.where(rows == w, 1.0, 0.0).astype(jnp.bfloat16) for w in wanted], axis=1)

    def spread_hot(to):
        base = to * HCAP
        wanted = []
        for table in range(TABLES):
            one = hot_pos[2 * table : 2 * table + 1, :] - base
            two = hot_pos[2 * table + 1 : 2 * table + 2, :] - base
            wanted.append(jnp.where((one >= 0) & (one < HCAP), one, two))
        return jnp.dot(
            one_hot(slot_id, wanted), terms[...], preferred_element_type=jnp.float32
        ).astype(jnp.bfloat16)

    half = MEMBERS // 2

    def spread_hot_send(i):
        to = members[i * 7 % MEMBERS]
        hot_send[i] = spread_hot(to)
        remote(
            hot_send.at[i], hot_got.at[i], send_sem.at[4], recv_sem.at[4 + i // half], (group, to)
        ).start()

    cold_wanted = [cold_pos[table : table + 1, :] for table in range(TABLES)]
    piece = MEMBERS // 2

    def spread_cold(k, target):
        for first in range(0, MEMBERS, piece):
            rows = jnp.concatenate(
                [
                    slot_id[:CCAP] + (to_group[k] * MEMBERS + members[i * 7 % MEMBERS]) * CCAP
                    for i in range(first, first + piece)
                ],
                axis=0,
            )
            sent = jnp.dot(
                one_hot(rows, cold_wanted), terms[...], preferred_element_type=jnp.float32
            )
            target[pl.ds(first, piece)] = sent.astype(jnp.bfloat16).reshape(piece, CCAP, LANES)

    for k in range(1, GROUPS):
        spread_hot_send(2 * k - 1)
        spread_hot_send(2 * k)
        spread_cold(k, cold_send.at[k])
        remote(
            cold_send.at[k], cold_mid.at[:, k], send_sem.at[5], recv_sem.at[9],
            (to_group[k], member),
        ).start()
    spread_hot_send(MEMBERS - 1)
    hot_got[0] = spread_hot(member)
    spread_cold(0, cold_mid.at[:, 0])

    def pass_cold(i, unused):
        to = to_member(i)
        remote(
            cold_mid.at[i], cold_got.at[pl.ds(i * GROUPS, GROUPS)], send_sem.at[9],
            cold_sem.at[lax.div(i, MEMBERS // WAVES)], (group, to),
        ).start()
        return unused

    def wide_sums(rows, ids, first, count, values):
        chosen = one_hot(rows, [ids[first + c] for c in range(count)])
        return jnp.dot(chosen, values[: count * LANES, :], preferred_element_type=jnp.float32)

    def widen(got, mask, first, count):
        for c in range(count):
            for q in range(CLASSES):
                wide_values[c * LANES : (c + 1) * LANES, q * LANES : (q + 1) * LANES] = (
                    got(c) * mask[q, first + c]
                )

    per_source = HCAP // LANES
    half_blocks = half * per_source

    def hot_part(first):
        def got(c):
            i, part = (first + c) // per_source, (first + c) % per_source
            return hot_got[i, part * LANES : (part + 1) * LANES, :]

        widen(got, hot_mask, first, half_blocks)

    def hot_rows_of(h):
        return jnp.concatenate(
            [row_id + h * LANES, row_id + (SLICE + h * LANES)], axis=0
        )

    drain(hot_got, 1, half - 1, send_sem.at[4], recv_sem.at[4]).wait_recv()
    hot_part(0)
    for h in range(2):
        sums = wide_sums(hot_rows_of(h), hot_ids, 0, half_blocks, wide_values)
        for g in range(GROUPS):
            partial[h, g] = sums[
                g % 2 * LANES : (g % 2 + 1) * LANES, g // 2 * LANES : (g // 2 + 1) * LANES
            ]
    drain(cold_got, 0, DEVICES - MEMBERS, send_sem.at[5], recv_sem.at[9]).wait_recv()
    lax.fori_loop(1, MEMBERS, pass_cold, 0)
    cold_got[pl.ds(0, GROUPS)] = cold_mid[0]
    drain(hot_got, half, MEMBERS - half, send_sem.at[4], recv_sem.at[5]).wait_recv()
    hot_part(half_blocks)
    for h in range(2):
        sums = wide_sums(hot_rows_of(h), hot_ids, half_blocks, half_blocks, wide_values)
        for g in range(GROUPS):
            total = partial[h, g] + sums[
                g % 2 * LANES : (g % 2 + 1) * LANES, g // 2 * LANES : (g // 2 + 1) * LANES
            ]
            partial[h, g] = total
            part_out[h, g] = total.astype(jnp.bfloat16)
        for k in range(1, GROUPS):
            remote(
                part_out.at[h, to_group[k]], part_got.at[h, k], send_sem.at[6], recv_sem.at[10 + h],
                (to_group[k], member),
            ).start()

    def share(h):
        part = part_got.at[h, pl.ds(1, GROUPS - 1)]
        remote(part, part, send_sem.at[6], recv_sem.at[10 + h], beside).wait_recv()
        total = partial[h, group]
        for k in range(1, GROUPS):
            total = total + part_got[h, k].astype(jnp.float32)
        own_grad[h] = total.astype(jnp.bfloat16)
        for k in range(1, GROUPS):
            remote(
                own_grad.at[h], hot_grad.at[group, h], send_sem.at[7], recv_sem.at[7],
                (to_group[k], member),
            ).start()

    block_rows = 512
    per_wave = DEVICES // WAVES
    wave_blocks = per_wave * CCAP // LANES
    big_id = lax.broadcasted_iota(jnp.int32, (block_rows, LANES), 0)

    def settle_cold(wave, waves):
        for n in range(wave, wave + waves):
            skip = GROUPS if n == 0 else 0
            drain(
                cold_got, n * per_wave + skip, per_wave - skip, send_sem.at[9], cold_sem.at[n]
            ).wait_recv()
        first, count = wave * wave_blocks, waves * wave_blocks

        def got(c):
            at = (first + c) * LANES // CCAP
            return cold_got[at : at + LANES // CCAP].reshape(LANES, LANES)

        widen(got, cold_mask, first, count)

        def block(n, unused):
            start = pl.multiple_of(n * block_rows, block_rows)
            sums = wide_sums(big_id + start, cold_ids, first, count, wide_values)
            for q in range(CLASSES):
                rows = pl.ds(start + q * COLD_CLASS, block_rows)
                part = sums[:, q * LANES : (q + 1) * LANES]
                cold_grad[rows, :] = part if wave == 0 else cold_grad[rows, :] + part
            return unused

        lax.fori_loop(0, COLD_CLASS // block_rows, block, 0)

    settle_cold(0, 2)
    share(0)
    settle_cold(2, 2)
    share(1)
    keep_own = load(own_grad, hot_grad.at[group], 15)
    settle_cold(4, 2)
    settle_cold(6, 1)
    settle_cold(7, 1)
    keep_cold = load(cold_grad, cold_grad_hbm, 16)
    keep_own.wait()
    keep_cold.wait()

    drain(hot_asked, 1, MEMBERS - 1, send_sem.at[0], recv_sem.at[0]).wait_send()
    drain(cold_asked, 0, DEVICES - MEMBERS, send_sem.at[1], recv_sem.at[1]).wait_send()
    drain(cold_asked, 0, DEVICES - GROUPS, send_sem.at[8], recv_sem.at[8]).wait_send()
    drain(hot_out, 1, MEMBERS - 1, send_sem.at[2], recv_sem.at[2]).wait_send()
    drain(cold_out, 1, DEVICES - 1, send_sem.at[3], recv_sem.at[3]).wait_send()
    drain(hot_send, 1, MEMBERS - 1, send_sem.at[4], recv_sem.at[4]).wait_send()
    drain(cold_got, 0, DEVICES - MEMBERS, send_sem.at[5], recv_sem.at[8]).wait_send()
    drain(cold_got, 0, DEVICES - GROUPS, send_sem.at[9], recv_sem.at[8]).wait_send()
    sent = part_out.at[:, pl.ds(1, GROUPS - 1)]
    remote(sent, sent, send_sem.at[6], recv_sem.at[6], beside).wait_send()
    drain(hot_grad, 1, GROUPS - 1, send_sem.at[7], recv_sem.at[7]).wait()


def train(
    hot_owner, hot_offset, cold_owner, cold_offset, bottom, labels, w_out,
    hot_table, cold_table, w_first, w_second,
):
    i32 = jnp.int32
    hot_block, cold_block = (MEMBERS, HCAP, LANES), (DEVICES, CCAP, LANES)
    return pl.pallas_call(
        step_kernel,
        out_shape=[
            jax.ShapeDtypeStruct((GROUPS, 2, LANES, LANES), jnp.bfloat16),
            jax.ShapeDtypeStruct((COLD_ROWS, LANES), jnp.float32),
        ],
        in_specs=[ANY] * 11,
        out_specs=[ANY] * 2,
        scratch_shapes=[
            pltpu.VMEM((2 * TABLES, LANES), i32), pltpu.VMEM((2 * TABLES, LANES), i32),
            pltpu.VMEM((TABLES, LANES), i32), pltpu.VMEM((TABLES, LANES), i32),
            f32(1, LANES), b16(*w_out.shape),
            pltpu.VMEM((MEMBERS, 1, HCAP), i32), pltpu.VMEM((DEVICES, 1, LANES), i32),
            pltpu.VMEM((2 * TABLES, LANES), i32), pltpu.VMEM((TABLES, LANES), i32),
            b16(2, LANES, LANES), f32(COLD_ROWS, LANES),
            f32(HOT_ROWS, LANES), f32(COLD_ROWS, LANES), b16(*w_first.shape), b16(*w_second.shape),
            pltpu.VMEM((MEMBERS, 1, HCAP), i32), pltpu.VMEM((DEVICES, 1, LANES), i32),
            pltpu.VMEM((MEMBERS, GROUPS, 1, LANES), i32), pltpu.SMEM((MEMBERS, 1, HCAP), i32), pltpu.SMEM((DEVICES, 1, LANES), i32),
            pltpu.SMEM((2 * TABLES, LANES), i32), pltpu.SMEM((TABLES, LANES), i32),
            b16(*hot_block), b16(*cold_block), b16(*hot_block), b16(*cold_block), f32(CCAP, LANES),
            f32(LANES, LANES), f32(MEMBERS * HCAP, LANES), f32(DEVICES * CCAP, LANES),
            b16(LANES, w_first.shape[0]), f32(TABLES, LANES, LANES), b16(PAIRS, LANES),
            b16(*hot_block), b16(GROUPS, MEMBERS, CCAP, LANES),
            b16(MEMBERS, GROUPS, CCAP, LANES), b16(*hot_block), b16(*cold_block),
            f32(2, GROUPS, LANES, LANES), b16(2, GROUPS, LANES, LANES), b16(2, GROUPS, LANES, LANES),
            pltpu.VMEM((MEMBERS * HCAP // LANES, 1, LANES), i32),
            pltpu.VMEM((DEVICES * CCAP // LANES, 1, LANES), i32),
            b16(CLASSES, MEMBERS * HCAP // LANES, LANES, LANES),
            b16(CLASSES, DEVICES * CCAP // LANES, LANES, LANES),
            b16(MEMBERS * HCAP // 2, CLASSES * LANES),
            DMA((17,)), DMA((10,)), DMA((12,)), DMA((WAVES,)), pltpu.SemaphoreType.REGULAR,
        ],
        compiler_params=pltpu.CompilerParams(
            collective_id=0, has_side_effects=True, vmem_limit_bytes=62 << 20
        ),
        name="step",
    )(
        hot_owner, hot_offset, cold_owner, cold_offset, bottom, labels, w_out,
        hot_table, cold_table, w_first, w_second,
    )


def update_kernel(
    hot_grad, hot_acc, hot_table, cold_grad, cold_acc, cold_table,
    new_hot, new_hot_acc, new_cold, new_cold_acc,
):
    first = lax.broadcasted_iota(jnp.int32, (LANES, LANES), 0)
    second = lax.broadcasted_iota(jnp.int32, (LANES, LANES), 1)
    diagonal = first == second

    def adagrad(gradient, acc, table, new_table, new_acc):
        for block in range(table.shape[0] // LANES):
            rows = slice(block * LANES, (block + 1) * LANES)
            grad = gradient[rows, :].astype(jnp.float32)
            spread_acc = jnp.where(diagonal, acc[0, block : block + 1, :], 0.0)
            new = jnp.sum(grad * grad * (1.0 / LANES) + spread_acc, axis=1, keepdims=True)
            new_table[rows, :] = table[rows, :] - STEP_RATE * grad * lax.rsqrt(new)
            new_acc[0, block : block + 1, :] = jnp.sum(
                jnp.where(diagonal, new, 0.0), axis=0, keepdims=True
            )

    adagrad(hot_grad, hot_acc, hot_table, new_hot, new_hot_acc)
    adagrad(cold_grad, cold_acc, cold_table, new_cold, new_cold_acc)


def update(hot_grad, hot_acc, hot_table, cold_grad, cold_acc, cold_table):
    steps = 2
    in_specs, out_specs, out_shape = [], [], []
    for table in (hot_table, cold_table):
        block = table.shape[0] // steps
        rows = pl.BlockSpec((block, LANES), lambda n: (n, 0))
        packed = pl.BlockSpec((1, block // LANES, LANES), lambda n: (n, 0, 0))
        in_specs += [rows, packed, rows]
        out_specs += [rows, packed]
        out_shape += [
            jax.ShapeDtypeStruct(table.shape, jnp.float32),
            jax.ShapeDtypeStruct((steps, block // LANES, LANES), jnp.float32),
        ]
    return pl.pallas_call(
        update_kernel,
        grid=(steps,),
        out_shape=out_shape,
        in_specs=in_specs,
        out_specs=out_specs,
        compiler_params=pltpu.CompilerParams(vmem_limit_bytes=62 << 20),
        name="update",
    )(
        hot_grad, hot_acc.reshape(steps, -1, LANES), hot_table,
        cold_grad, cold_acc.reshape(steps, -1, LANES), cold_table,
    )


def shards(
    hot_table, hot_acc, cold_table, cold_acc, bottom_out, labels,
    hot_owner, hot_offset, cold_owner, cold_offset, w_first, w_second, w_out,
):
    def by_lane(lookups):
        return jnp.transpose(lookups, (1, 2, 0)).reshape(-1, LANES)

    hot_grad, cold_grad = train(
        by_lane(hot_owner), by_lane(hot_offset), by_lane(cold_owner), by_lane(cold_offset),
        bottom_out, labels.reshape(1, -1), w_out, hot_table, cold_table, w_first, w_second,
    )
    new_hot, new_hot_acc, new_cold, new_cold_acc = update(
        hot_grad.reshape(-1, LANES), hot_acc, hot_table, cold_grad, cold_acc, cold_table
    )
    return (new_hot, new_hot_acc.reshape(-1), new_cold, new_cold_acc.reshape(-1))


def solution(mesh):
    both = P(("group", "member"))
    in_specs = (P("member"), P("member")) + (both,) * 8 + (P(),) * 3
    out_specs = (P("member"), P("member"), both, both)
    return jax.shard_map(shards, mesh=mesh, in_specs=in_specs, out_specs=out_specs, check_vma=False)
```

```python
import functools

import jax
import jax.numpy as jnp
from jax import lax
from jax.experimental import pallas as pl
from jax.experimental.pallas import tpu as pltpu
from jax.sharding import PartitionSpec as P

STEP_RATE = 0.5
LANES = 128
MEMBERS = 16
GROUPS = 8
DEVICES = 128
HOT_ROWS = 2048
COLD_ROWS = 4096
HCAP = 256
CCAP = 32
HIDDEN = 2048
TABLES = 8
SLICE = HOT_ROWS // GROUPS
MESH = pl.DeviceIdType.MESH
NT = (((1,), (1,)), ((), ()))

ANY = pl.BlockSpec(memory_space=pl.ANY)
DMA = pltpu.SemaphoreType.DMA


def f32(*shape):
    return pltpu.VMEM(shape, jnp.float32)


def b16(*shape):
    return pltpu.VMEM(shape, jnp.bfloat16)


def remote(src, dst, send, recv, to):
    return pltpu.make_async_remote_copy(
        src_ref=src, dst_ref=dst, send_sem=send, recv_sem=recv, device_id=to, device_id_type=MESH
    )


def place(owner_ref, offset_ref, owners, cap, table_rows, request_ref, position_ref):
    rows = owner_ref.shape[0]
    owner_ids = lax.broadcasted_iota(jnp.int32, (owners, LANES), 0)
    hits = [(owner_ref[r : r + 1, :] == owner_ids).astype(jnp.float32) for r in range(rows)]
    stacked = jnp.concatenate(hits, axis=0).astype(jnp.bfloat16)
    first = lax.broadcasted_iota(jnp.int32, (LANES, LANES), 0)
    second = lax.broadcasted_iota(jnp.int32, (LANES, LANES), 1)
    earlier = (first < second).astype(jnp.float32)
    side = jnp.concatenate([earlier, jnp.ones((LANES, LANES), jnp.float32)], axis=1)
    counts = jnp.dot(stacked, side.astype(jnp.bfloat16), preferred_element_type=jnp.float32)
    base = jnp.zeros((owners, LANES), jnp.float32)
    width = request_ref.shape[2]
    slots = lax.broadcasted_iota(jnp.int32, (width, LANES), 0) % cap
    high, low, at_slot = [], [], []
    for r in range(rows):
        count = counts[r * owners : (r + 1) * owners]
        slot = jnp.sum(hits[r] * (count[:, :LANES] + base), axis=0, keepdims=True).astype(jnp.int32)
        base = base + count[:, LANES:]
        position_ref[r : r + 1, :] = jnp.clip(
            owner_ref[r : r + 1, :] * cap + slot, 0, owners * cap - 1
        )
        offset = offset_ref[r : r + 1, :]
        high.append(hits[r] * (offset // 64).astype(jnp.float32))
        low.append(hits[r] * (offset % 64).astype(jnp.float32))
        at_slot.append((slots == slot).astype(jnp.float32).astype(jnp.bfloat16))
    digits = jnp.concatenate(
        [jnp.concatenate(high, axis=1), jnp.concatenate(low, axis=1)], axis=0
    ).astype(jnp.bfloat16)
    placed = lax.dot_general(
        digits, jnp.concatenate(at_slot, axis=1), NT, preferred_element_type=jnp.float32
    )
    requests = jnp.clip(
        (placed[:owners] * 64.0 + placed[owners:]).astype(jnp.int32), 0, table_rows - 1
    )
    for owner in range(owners):
        request_ref[owner] = requests[owner : owner + 1, :]


WAVES = 8
CLASSES = 4
HOT_CLASS = HOT_ROWS // CLASSES
COLD_CLASS = COLD_ROWS // CLASSES
PAIRS = TABLES * LANES


def step_kernel(
    hot_owner_hbm, hot_offset_hbm, cold_owner_hbm, cold_offset_hbm, bottom_hbm, labels_hbm, out_hbm,
    hot_hbm, cold_hbm, first_hbm, second_hbm,
    hot_grad, cold_grad_hbm,
    hot_owner, hot_offset, cold_owner, cold_offset, labels, w_out,
    hot_request, cold_request, hot_pos, cold_pos, own_grad, cold_grad,
    hot_table, cold_table, w_first, w_second,
    hot_asked, cold_asked, cold_asked_mid, hot_index, cold_index, hot_at, cold_at,
    hot_out, cold_out, hot_rows, cold_rows, stage, picked, hot_wide, cold_wide, features, pooled, terms,
    hot_send, cold_send, cold_mid, hot_got, cold_got, partial, part_out, part_got,
    hot_ids, cold_ids, hot_mask, cold_mask, wide_values,
    local_sem, send_sem, recv_sem, cold_sem, present,
):
    group, member = lax.axis_index("group"), lax.axis_index("member")
    me = group * MEMBERS + member
    z, x, y, core = lax.div(member, 4), lax.rem(member, 4), lax.div(group, 2), lax.rem(group, 2)
    xs = [lax.rem(x + d, 4) for d in range(4)]
    zs = [lax.rem(z + d, 4) * 4 for d in range(4)]
    members = [zs[d // 4] + xs[d % 4] for d in range(MEMBERS)]
    ys = [lax.rem(y + d, 4) * 2 for d in range(4)]
    cores = [core, 1 - core]
    to_group = [ys[k // 2] + cores[k % 2] for k in range(GROUPS)]
    from_group = [ys[(4 - k // 2) % 4] + cores[k % 2] for k in range(GROUPS)]

    def member_step(i):
        step = lax.rem(i * 7, MEMBERS)
        return lax.div(step, 4), lax.rem(step, 4)

    def to_member(i):
        dz, dx = member_step(i)
        return lax.rem(z + dz, 4) * 4 + lax.rem(x + dx, 4)

    def from_member(i):
        dz, dx = member_step(i)
        return lax.rem(z + 4 - dz, 4) * 4 + lax.rem(x + 4 - dx, 4)

    def load(src, dst, n):
        copy = pltpu.make_async_copy(src, dst, local_sem.at[n])
        copy.start()
        return copy

    ids = [
        load(hot_owner_hbm, hot_owner, 0), load(hot_offset_hbm, hot_offset, 1),
        load(cold_owner_hbm, cold_owner, 2), load(cold_offset_hbm, cold_offset, 3),
    ]
    barrier = pltpu.get_barrier_semaphore()
    for d in range(1, MEMBERS):
        pl.semaphore_signal(barrier, inc=1, device_id=(group, members[d]), device_id_type=MESH)
    for k in range(1, GROUPS):
        pl.semaphore_signal(barrier, inc=1, device_id=(to_group[k], member), device_id_type=MESH)
    load_hot = load(hot_hbm, hot_table, 4)
    load_cold = load(cold_hbm, cold_table, 5)
    small = [
        load(bottom_hbm, features.at[:, pl.ds(0, LANES)], 6), load(labels_hbm, labels, 7),
        load(out_hbm, w_out, 8),
    ]
    load_first = load(first_hbm, w_first, 9)
    load_second = load(second_hbm, w_second, 10)
    ids[0].wait()
    ids[1].wait()
    place(hot_owner, hot_offset, MEMBERS, HCAP, HOT_ROWS, hot_request, hot_pos)
    pl.semaphore_wait(barrier, MEMBERS - 1 + GROUPS - 1)
    for k in range(1, GROUPS):
        pl.semaphore_signal(present, inc=1, device_id=(to_group[k], member), device_id_type=MESH)

    beside = (group, members[1])

    def drain(buffer, first, parts, send, recv):
        part = buffer.at[pl.ds(first, parts)]
        return remote(part, part, send, recv, beside)

    def ask_hot(i, unused):
        to = to_member(i)
        remote(
            hot_request.at[to], hot_asked.at[i], send_sem.at[0], recv_sem.at[0], (group, to)
        ).start()
        return unused

    lax.fori_loop(1, MEMBERS, ask_hot, 0)
    hot_asked[0] = hot_request[member]
    ids[2].wait()
    ids[3].wait()
    place(cold_owner, cold_offset, DEVICES, CCAP, COLD_ROWS, cold_request, cold_pos)
    index_loads = [load(hot_pos, hot_at, 11), load(cold_pos, cold_at, 12)]
    for k in range(1, GROUPS):
        remote(
            cold_request.at[pl.ds(to_group[k] * MEMBERS, MEMBERS)], cold_asked_mid.at[:, k],
            send_sem.at[1], recv_sem.at[1], (to_group[k], member),
        ).start()
    cold_asked_mid[:, 0] = cold_request[pl.ds(group * MEMBERS, MEMBERS)]

    drain(hot_asked, 1, MEMBERS - 1, send_sem.at[0], recv_sem.at[0]).wait_recv()
    to_scalars = load(hot_asked, hot_index, 13)
    load_hot.wait()
    to_scalars.wait()

    def pick(table, index, row, first, target):
        for j in range(CCAP):
            stage[pl.ds(j, 1), :] = table[pl.ds(index[row, 0, first + j], 1), :]
        target[...] = stage[...].astype(jnp.bfloat16)

    def serve_hot(i, target):
        def chunk(c, unused):
            first = pl.multiple_of(c * CCAP, CCAP)
            pick(hot_table, hot_index, i, first, target.at[pl.ds(first, CCAP), :])
            return unused

        lax.fori_loop(0, HCAP // CCAP, chunk, 0)

    def serve_hot_send(i, unused):
        to = from_member(i)
        serve_hot(i, hot_out.at[i])
        remote(
            hot_out.at[i], hot_rows.at[member], send_sem.at[2], recv_sem.at[2], (group, to)
        ).start()
        return unused

    def ask_cold(i, unused):
        to = to_member(i)
        remote(
            cold_asked_mid.at[to], cold_asked.at[pl.ds(i * GROUPS, GROUPS)],
            send_sem.at[8], recv_sem.at[8], (group, to),
        ).start()
        return unused

    lax.fori_loop(1, 5, serve_hot_send, 0)
    drain(cold_asked, 0, DEVICES - MEMBERS, send_sem.at[1], recv_sem.at[1]).wait_recv()
    lax.fori_loop(1, MEMBERS, ask_cold, 0)
    cold_asked[pl.ds(0, GROUPS)] = cold_asked_mid[member]
    lax.fori_loop(5, MEMBERS, serve_hot_send, 0)
    serve_hot(0, hot_rows.at[member])

    drain(cold_asked, 0, DEVICES - GROUPS, send_sem.at[8], recv_sem.at[8]).wait_recv()
    to_scalars = load(cold_asked, cold_index, 14)
    load_cold.wait()
    to_scalars.wait()
    pl.semaphore_wait(present, GROUPS - 1)

    def serve_cold_at(i, groups):
        to = from_member(i)
        for k in groups:
            n = i * GROUPS + k
            pick(cold_table, cold_index, n, 0, cold_out.at[n])
            remote(
                cold_out.at[n], cold_rows.at[me], send_sem.at[3], recv_sem.at[3],
                (from_group[k], to),
            ).start()

    def serve_cold(i, unused):
        serve_cold_at(i, range(GROUPS))
        return unused

    serve_cold_at(0, range(1, GROUPS))
    lax.fori_loop(1, MEMBERS, serve_cold, 0)
    pick(cold_table, cold_index, 0, 0, cold_rows.at[me])

    row_id = lax.broadcasted_iota(jnp.int32, (LANES, LANES), 0)
    lane_id = lax.broadcasted_iota(jnp.int32, (LANES, LANES), 1)
    diagonal = row_id == lane_id
    ones = jnp.ones((LANES, LANES), jnp.bfloat16)
    quarter = lax.div(lax.broadcasted_iota(jnp.int32, (1, LANES), 1), CCAP)

    def note(asked, size, n, ids, mask):
        ids[n] = lax.rem(asked, size)
        which = lax.div(asked, size).astype(jnp.float32)
        wide = jnp.dot(
            jnp.where(diagonal, which, 0.0).astype(jnp.bfloat16), ones,
            preferred_element_type=jnp.float32,
        )
        for q in range(CLASSES):
            mask[q, n] = jnp.where(wide == q, 1.0, 0.0).astype(jnp.bfloat16)

    together = 4

    def note_some(step, unused):
        for j in range(together):
            n = step * together + j
            asked = hot_asked[step * (together // 2) + j // 2]
            asked = asked[:, j % 2 * LANES : (j % 2 + 1) * LANES]
            note(asked, HOT_CLASS, n, hot_ids, hot_mask)
            asked = cold_asked[4 * n]
            for q in range(1, 4):
                asked = jnp.where(quarter == q, cold_asked[4 * n + q], asked)
            note(asked, COLD_CLASS, n, cold_ids, cold_mask)
        return unused

    lax.fori_loop(0, DEVICES // 4 // together, note_some, 0)

    for copy in index_loads + small:
        copy.wait()
    unroll = 16
    drain(hot_rows, 0, MEMBERS - 1, send_sem.at[2], recv_sem.at[2]).wait_recv()
    hot_wide[...] = hot_rows[...].astype(jnp.float32).reshape(hot_wide.shape)
    for table in range(TABLES):

        def combine_hot(k, unused):
            for j in range(unroll):
                b = k * unroll + j
                pooled[table, pl.ds(b, 1), :] = (
                    hot_wide[pl.ds(hot_at[2 * table, b], 1), :]
                    + hot_wide[pl.ds(hot_at[2 * table + 1, b], 1), :]
                )
            return unused

        lax.fori_loop(0, LANES // unroll, combine_hot, 0)
    drain(cold_rows, 0, DEVICES - 1, send_sem.at[3], recv_sem.at[3]).wait_recv()
    cold_wide[...] = cold_rows[...].astype(jnp.float32).reshape(cold_wide.shape)
    for table in range(TABLES):

        def combine_cold(k, unused):
            for j in range(unroll):
                b = k * unroll + j
                picked[pl.ds(b, 1), :] = cold_wide[pl.ds(cold_at[table, b], 1), :]
            return unused

        lax.fori_loop(0, LANES // unroll, combine_cold, 0)
        features[:, (table + 1) * LANES : (table + 2) * LANES] = (
            pooled[table] + picked[...]
        ).astype(jnp.bfloat16)

    load_first.wait()
    first_pre = jnp.dot(features[...], w_first[...], preferred_element_type=jnp.float32)
    first_act = jnp.maximum(first_pre, 0.0).astype(jnp.bfloat16)
    load_second.wait()
    second_pre = jnp.dot(first_act, w_second[...], preferred_element_type=jnp.float32)
    second_act = jnp.maximum(second_pre, 0.0).astype(jnp.bfloat16)
    out_wide = w_out[...].astype(jnp.float32).reshape(1, -1)
    score = jnp.sum(second_act.astype(jnp.float32) * out_wide, axis=1, keepdims=True)
    label = jnp.sum(jnp.where(diagonal, labels[...], 0.0), axis=1, keepdims=True)
    delta = jax.nn.sigmoid(score) - label
    grad_second = jnp.where(second_pre > 0, delta * out_wide, 0.0).astype(jnp.bfloat16)
    back_second = lax.dot_general(grad_second, w_second[...], NT, preferred_element_type=jnp.float32)
    grad_first = jnp.where(first_pre > 0, back_second, 0.0).astype(jnp.bfloat16)
    for table in range(TABLES):
        terms[table * LANES : (table + 1) * LANES, :] = lax.dot_general(
            grad_first, w_first[(table + 1) * LANES : (table + 2) * LANES, :], NT,
            preferred_element_type=jnp.float32,
        ).astype(jnp.bfloat16)

    slot_id = lax.broadcasted_iota(jnp.int32, (HCAP, LANES), 0)

    def one_hot(rows, wanted):
        return jnp.concatenate([jnp.where(rows == w, 1.0, 0.0).astype(jnp.bfloat16) for w in wanted], axis=1)

    def spread_hot(to):
        base = to * HCAP
        wanted = []
        for table in range(TABLES):
            one = hot_pos[2 * table : 2 * table + 1, :] - base
            two = hot_pos[2 * table + 1 : 2 * table + 2, :] - base
            wanted.append(jnp.where((one >= 0) & (one < HCAP), one, two))
        return jnp.dot(
            one_hot(slot_id, wanted), terms[...], preferred_element_type=jnp.float32
        ).astype(jnp.bfloat16)

    half = MEMBERS // 2

    def spread_hot_send(i):
        to = members[i * 7 % MEMBERS]
        hot_send[i] = spread_hot(to)
        remote(
            hot_send.at[i], hot_got.at[i], send_sem.at[4], recv_sem.at[4 + i // half], (group, to)
        ).start()

    cold_wanted = [cold_pos[table : table + 1, :] for table in range(TABLES)]
    piece = MEMBERS // 2

    def spread_cold(k, target):
        for first in range(0, MEMBERS, piece):
            rows = jnp.concatenate(
                [
                    slot_id[:CCAP] + (to_group[k] * MEMBERS + members[i * 7 % MEMBERS]) * CCAP
                    for i in range(first, first + piece)
                ],
                axis=0,
            )
            sent = jnp.dot(
                one_hot(rows, cold_wanted), terms[...], preferred_element_type=jnp.float32
            )
            target[pl.ds(first, piece)] = sent.astype(jnp.bfloat16).reshape(piece, CCAP, LANES)

    for k in range(1, GROUPS):
        spread_hot_send(2 * k - 1)
        spread_hot_send(2 * k)
        spread_cold(k, cold_send.at[k])
        remote(
            cold_send.at[k], cold_mid.at[:, k], send_sem.at[5], recv_sem.at[9],
            (to_group[k], member),
        ).start()
    spread_hot_send(MEMBERS - 1)
    hot_got[0] = spread_hot(member)
    spread_cold(0, cold_mid.at[:, 0])

    def pass_cold(i, unused):
        to = to_member(i)
        remote(
            cold_mid.at[i], cold_got.at[pl.ds(i * GROUPS, GROUPS)], send_sem.at[9],
            cold_sem.at[lax.div(i, MEMBERS // WAVES)], (group, to),
        ).start()
        return unused

    def wide_sums(rows, ids, first, count, values):
        chosen = one_hot(rows, [ids[first + c] for c in range(count)])
        return jnp.dot(chosen, values[: count * LANES, :], preferred_element_type=jnp.float32)

    def widen(got, mask, first, count):
        for c in range(count):
            for q in range(CLASSES):
                wide_values[c * LANES : (c + 1) * LANES, q * LANES : (q + 1) * LANES] = (
                    got(c) * mask[q, first + c]
                )

    per_source = HCAP // LANES
    half_blocks = half * per_source

    def hot_part(first):
        def got(c):
            i, part = (first + c) // per_source, (first + c) % per_source
            return hot_got[i, part * LANES : (part + 1) * LANES, :]

        widen(got, hot_mask, first, half_blocks)

    def hot_rows_of(h):
        return jnp.concatenate(
            [row_id + h * LANES, row_id + (SLICE + h * LANES)], axis=0
        )

    drain(hot_got, 1, half - 1, send_sem.at[4], recv_sem.at[4]).wait_recv()
    hot_part(0)
    for h in range(2):
        sums = wide_sums(hot_rows_of(h), hot_ids, 0, half_blocks, wide_values)
        for g in range(GROUPS):
            partial[h, g] = sums[
                g % 2 * LANES : (g % 2 + 1) * LANES, g // 2 * LANES : (g // 2 + 1) * LANES
            ]
    drain(cold_got, 0, DEVICES - MEMBERS, send_sem.at[5], recv_sem.at[9]).wait_recv()
    lax.fori_loop(1, MEMBERS, pass_cold, 0)
    cold_got[pl.ds(0, GROUPS)] = cold_mid[0]
    drain(hot_got, half, MEMBERS - half, send_sem.at[4], recv_sem.at[5]).wait_recv()
    hot_part(half_blocks)
    for h in range(2):
        sums = wide_sums(hot_rows_of(h), hot_ids, half_blocks, half_blocks, wide_values)
        for g in range(GROUPS):
            total = partial[h, g] + sums[
                g % 2 * LANES : (g % 2 + 1) * LANES, g // 2 * LANES : (g // 2 + 1) * LANES
            ]
            partial[h, g] = total
            part_out[h, g] = total.astype(jnp.bfloat16)
        for k in range(1, GROUPS):
            remote(
                part_out.at[h, to_group[k]], part_got.at[h, k], send_sem.at[6], recv_sem.at[10 + h],
                (to_group[k], member),
            ).start()

    def share(h):
        part = part_got.at[h, pl.ds(1, GROUPS - 1)]
        remote(part, part, send_sem.at[6], recv_sem.at[10 + h], beside).wait_recv()
        total = partial[h, group]
        for k in range(1, GROUPS):
            total = total + part_got[h, k].astype(jnp.float32)
        own_grad[h] = total.astype(jnp.bfloat16)
        for k in range(1, GROUPS):
            remote(
                own_grad.at[h], hot_grad.at[group, h], send_sem.at[7], recv_sem.at[7],
                (to_group[k], member),
            ).start()

    block_rows = 512
    per_wave = DEVICES // WAVES
    wave_blocks = per_wave * CCAP // LANES
    big_id = lax.broadcasted_iota(jnp.int32, (block_rows, LANES), 0)

    def settle_cold(wave, waves):
        for n in range(wave, wave + waves):
            skip = GROUPS if n == 0 else 0
            drain(
                cold_got, n * per_wave + skip, per_wave - skip, send_sem.at[9], cold_sem.at[n]
            ).wait_recv()
        first, count = wave * wave_blocks, waves * wave_blocks

        def got(c):
            at = (first + c) * LANES // CCAP
            return cold_got[at : at + LANES // CCAP].reshape(LANES, LANES)

        widen(got, cold_mask, first, count)

        def block(n, unused):
            start = pl.multiple_of(n * block_rows, block_rows)
            sums = wide_sums(big_id + start, cold_ids, first, count, wide_values)
            for q in range(CLASSES):
                rows = pl.ds(start + q * COLD_CLASS, block_rows)
                part = sums[:, q * LANES : (q + 1) * LANES]
                cold_grad[rows, :] = part if wave == 0 else cold_grad[rows, :] + part
            return unused

        lax.fori_loop(0, COLD_CLASS // block_rows, block, 0)

    settle_cold(0, 2)
    share(0)
    settle_cold(2, 2)
    share(1)
    keep_own = load(own_grad, hot_grad.at[group], 15)
    settle_cold(4, 2)
    settle_cold(6, 1)
    settle_cold(7, 1)
    keep_cold = load(cold_grad, cold_grad_hbm, 16)
    keep_own.wait()
    keep_cold.wait()

    drain(hot_asked, 1, MEMBERS - 1, send_sem.at[0], recv_sem.at[0]).wait_send()
    drain(cold_asked, 0, DEVICES - MEMBERS, send_sem.at[1], recv_sem.at[1]).wait_send()
    drain(cold_asked, 0, DEVICES - GROUPS, send_sem.at[8], recv_sem.at[8]).wait_send()
    drain(hot_out, 1, MEMBERS - 1, send_sem.at[2], recv_sem.at[2]).wait_send()
    drain(cold_out, 1, DEVICES - 1, send_sem.at[3], recv_sem.at[3]).wait_send()
    drain(hot_send, 1, MEMBERS - 1, send_sem.at[4], recv_sem.at[4]).wait_send()
    drain(cold_got, 0, DEVICES - MEMBERS, send_sem.at[5], recv_sem.at[8]).wait_send()
    drain(cold_got, 0, DEVICES - GROUPS, send_sem.at[9], recv_sem.at[8]).wait_send()
    sent = part_out.at[:, pl.ds(1, GROUPS - 1)]
    remote(sent, sent, send_sem.at[6], recv_sem.at[6], beside).wait_send()
    drain(hot_grad, 1, GROUPS - 1, send_sem.at[7], recv_sem.at[7]).wait()


def train(
    hot_owner, hot_offset, cold_owner, cold_offset, bottom, labels, w_out,
    hot_table, cold_table, w_first, w_second,
):
    i32 = jnp.int32
    hot_block, cold_block = (MEMBERS, HCAP, LANES), (DEVICES, CCAP, LANES)
    return pl.pallas_call(
        step_kernel,
        out_shape=[
            jax.ShapeDtypeStruct((GROUPS, 2, LANES, LANES), jnp.bfloat16),
            jax.ShapeDtypeStruct((COLD_ROWS, LANES), jnp.float32),
        ],
        in_specs=[ANY] * 11,
        out_specs=[ANY] * 2,
        scratch_shapes=[
            pltpu.VMEM((2 * TABLES, LANES), i32), pltpu.VMEM((2 * TABLES, LANES), i32),
            pltpu.VMEM((TABLES, LANES), i32), pltpu.VMEM((TABLES, LANES), i32),
            f32(1, LANES), b16(*w_out.shape),
            pltpu.VMEM((MEMBERS, 1, HCAP), i32), pltpu.VMEM((DEVICES, 1, LANES), i32),
            pltpu.VMEM((2 * TABLES, LANES), i32), pltpu.VMEM((TABLES, LANES), i32),
            b16(2, LANES, LANES), f32(COLD_ROWS, LANES),
            f32(HOT_ROWS, LANES), f32(COLD_ROWS, LANES), b16(*w_first.shape), b16(*w_second.shape),
            pltpu.VMEM((MEMBERS, 1, HCAP), i32), pltpu.VMEM((DEVICES, 1, LANES), i32),
            pltpu.VMEM((MEMBERS, GROUPS, 1, LANES), i32), pltpu.SMEM((MEMBERS, 1, HCAP), i32), pltpu.SMEM((DEVICES, 1, LANES), i32),
            pltpu.SMEM((2 * TABLES, LANES), i32), pltpu.SMEM((TABLES, LANES), i32),
            b16(*hot_block), b16(*cold_block), b16(*hot_block), b16(*cold_block), f32(CCAP, LANES),
            f32(LANES, LANES), f32(MEMBERS * HCAP, LANES), f32(DEVICES * CCAP, LANES),
            b16(LANES, w_first.shape[0]), f32(TABLES, LANES, LANES), b16(PAIRS, LANES),
            b16(*hot_block), b16(GROUPS, MEMBERS, CCAP, LANES),
            b16(MEMBERS, GROUPS, CCAP, LANES), b16(*hot_block), b16(*cold_block),
            f32(2, GROUPS, LANES, LANES), b16(2, GROUPS, LANES, LANES), b16(2, GROUPS, LANES, LANES),
            pltpu.VMEM((MEMBERS * HCAP // LANES, 1, LANES), i32),
            pltpu.VMEM((DEVICES * CCAP // LANES, 1, LANES), i32),
            b16(CLASSES, MEMBERS * HCAP // LANES, LANES, LANES),
            b16(CLASSES, DEVICES * CCAP // LANES, LANES, LANES),
            b16(MEMBERS * HCAP // 2, CLASSES * LANES),
            DMA((17,)), DMA((10,)), DMA((12,)), DMA((WAVES,)), pltpu.SemaphoreType.REGULAR,
        ],
        compiler_params=pltpu.CompilerParams(
            collective_id=0, has_side_effects=True, vmem_limit_bytes=62 << 20
        ),
        name="step",
    )(
        hot_owner, hot_offset, cold_owner, cold_offset, bottom, labels, w_out,
        hot_table, cold_table, w_first, w_second,
    )


def update_kernel(
    hot_grad, hot_acc, hot_table, cold_grad, cold_acc, cold_table,
    new_hot, new_hot_acc, new_cold, new_cold_acc,
):
    first = lax.broadcasted_iota(jnp.int32, (LANES, LANES), 0)
    second = lax.broadcasted_iota(jnp.int32, (LANES, LANES), 1)
    diagonal = first == second

    def adagrad(gradient, acc, table, new_table, new_acc):
        for block in range(table.shape[0] // LANES):
            rows = slice(block * LANES, (block + 1) * LANES)
            grad = gradient[rows, :].astype(jnp.float32)
            spread_acc = jnp.where(diagonal, acc[0, block : block + 1, :], 0.0)
            new = jnp.sum(grad * grad * (1.0 / LANES) + spread_acc, axis=1, keepdims=True)
            new_table[rows, :] = table[rows, :] - STEP_RATE * grad * lax.rsqrt(new)
            new_acc[0, block : block + 1, :] = jnp.sum(
                jnp.where(diagonal, new, 0.0), axis=0, keepdims=True
            )

    adagrad(hot_grad, hot_acc, hot_table, new_hot, new_hot_acc)
    adagrad(cold_grad, cold_acc, cold_table, new_cold, new_cold_acc)


def update(hot_grad, hot_acc, hot_table, cold_grad, cold_acc, cold_table):
    steps = 2
    in_specs, out_specs, out_shape = [], [], []
    for table in (hot_table, cold_table):
        block = table.shape[0] // steps
        rows = pl.BlockSpec((block, LANES), lambda n: (n, 0))
        packed = pl.BlockSpec((1, block // LANES, LANES), lambda n: (n, 0, 0))
        in_specs += [rows, packed, rows]
        out_specs += [rows, packed]
        out_shape += [
            jax.ShapeDtypeStruct(table.shape, jnp.float32),
            jax.ShapeDtypeStruct((steps, block // LANES, LANES), jnp.float32),
        ]
    return pl.pallas_call(
        update_kernel,
        grid=(steps,),
        out_shape=out_shape,
        in_specs=in_specs,
        out_specs=out_specs,
        compiler_params=pltpu.CompilerParams(vmem_limit_bytes=62 << 20),
        name="update",
    )(
        hot_grad, hot_acc.reshape(steps, -1, LANES), hot_table,
        cold_grad, cold_acc.reshape(steps, -1, LANES), cold_table,
    )


def shards(
    hot_table, hot_acc, cold_table, cold_acc, bottom_out, labels,
    hot_owner, hot_offset, cold_owner, cold_offset, w_first, w_second, w_out,
):
    def by_lane(lookups):
        return jnp.transpose(lookups, (1, 2, 0)).reshape(-1, LANES)

    hot_grad, cold_grad = train(
        by_lane(hot_owner), by_lane(hot_offset), by_lane(cold_owner), by_lane(cold_offset),
        bottom_out, labels.reshape(1, -1), w_out, hot_table, cold_table, w_first, w_second,
    )
    new_hot, new_hot_acc, new_cold, new_cold_acc = update(
        hot_grad.reshape(-1, LANES), hot_acc, hot_table, cold_grad, cold_acc, cold_table
    )
    return (new_hot, new_hot_acc.reshape(-1), new_cold, new_cold_acc.reshape(-1))


def solution(mesh):
    both = P(("group", "member"))
    in_specs = (P("member"), P("member")) + (both,) * 8 + (P(),) * 3
    out_specs = (P("member"), P("member"), both, both)
    return jax.shard_map(shards, mesh=mesh, in_specs=in_specs, out_specs=out_specs, check_vma=False)
```
